256 devices in a mesh: rows: 32 (over z_hi, x, core), cols: 8 (over y, z_lo).
Axes of the slice: x: 4, y: 4, z: 8 (z_hi: 4, z_lo: 2; z = z_hi * 2 + z_lo), core: 2. Of those that a mesh axis runs over, the one named last changes fastest.
Arguments:
- xin: bfloat16 [256, 512, 1024], P('rows', 'cols'), may hold values from -6 to 6
- gate_in: bfloat16 [256, 512, 1024], P('rows', 'cols'), may hold values from -6 to 6
- w_proj: bfloat16 [1024, 128], replicated, may hold values from -0.1875 to 0.1875
- rate: float32 [4, 16], replicated, may hold values from 0.0001953125 to 0.05
- skip: float32 [1024], replicated, may hold values from 0.5 to 1.5
- norm_gain: float32 [1024], replicated, may hold values from 0.5 to 1.5
- w_out: bfloat16 [1024, 512], replicated, may hold values from -0.1875 to 0.1875
Outputs:
- mixed: bfloat16 [256, 512, 512], P('rows', 'cols')
The draws below stay inside these ranges and needn't reach their ends.
All inputs are finite; a program needn't handle non-finite values.
Results may differ from the reference program's by a relative error of at most 0.0049.
Values sent between devices are 32-bit elements; how exact they have to be, the bound alone decides.
A program may use at most 192 MiB of HBM per device.

```python
import jax
import jax.numpy as jnp
from jax import lax

E = 1024
D = 512
HEADS = 16
PROJ = 128
H_IMG = 256
W_IMG = 512


def draw_rate(key, part):
    key = jax.random.fold_in(key, 7)
    first, second = jax.random.split(key, 2)
    lengths = jnp.array([W_IMG, W_IMG, H_IMG, H_IMG], jnp.float32)[:, None]
    unit = jax.random.uniform(first, (4, HEADS), jnp.float32)
    slow = jnp.exp(jnp.log(0.1) + unit * jnp.log(20.0)) / lengths
    fast = jnp.exp(jnp.log(0.02) + unit * jnp.log(2.5))
    picks = jax.random.randint(second, (4, HEADS), 0, 2) == 1
    lowest = 0.1 / max(H_IMG, W_IMG)
    return jnp.clip(jnp.where(picks, fast, slow), lowest, 0.05).astype(jnp.float32)


def level_of(own_key, shape, shards, smallest, top_value):
    level, own = 1.0, jax.random.fold_in(own_key, 6)
    for dim, parts in shards:
        steps = jnp.exp(jax.random.uniform(jax.random.fold_in(own, dim), (parts,), jnp.float32, smallest / len(shards), top_value / len(shards)))
        level = level * jnp.repeat(steps, shape[dim] // parts).reshape([-1 if axis == dim else 1 for axis in range(len(shape))])
    return level


def centred(key, shape, spread, most, pieces=(), kind=jnp.bfloat16):
    loudness = level_of(key, shape, pieces, -0.22, 0.18) if pieces else 1.0
    values = jax.random.normal(key, shape, jnp.float32) * spread * loudness
    return jnp.minimum(jnp.maximum(values, -most), most).astype(kind)


def setup_inputs(seed: int = 0) -> dict:
    splits = jax.random.split(jax.random.key(seed), 8)
    return {
        "xin": centred(splits[0], (H_IMG, W_IMG, E), 1.0, 6.0, ((0, 32), (1, 8))),
        "gate_in": centred(splits[1], (H_IMG, W_IMG, E), 1.0, 6.0, ((0, 32), (1, 8))),
        "w_proj": centred(splits[2], (E, PROJ), E ** -0.5, 0.1875),
        "rate": draw_rate(jax.random.fold_in(splits[7], 71), 0),
        "skip": jnp.clip(jax.random.uniform(splits[4], (E,), jnp.float32, 0.5, 1.5), 0.5, 1.5),
        "norm_gain": jnp.clip(1.0 + 0.1 * jax.random.normal(splits[5], (E,), jnp.float32), 0.5, 1.5),
        "w_out": centred(splits[6], (E, D), E ** -0.5, 0.1875),
    }


def scan_lines(decay, drive, outcoef, backward):

    def advance(state, items):
        factor, push, weight = items
        state = factor[:, None] * state + push
        return (state, weight[:, None] * state)
    start = jnp.zeros(drive.shape[1:], jnp.float32)
    _, outputs = lax.scan(advance, start, (decay, drive, outcoef), reverse=backward)
    return outputs

def reference(xin, gate_in, w_proj, rate, skip, norm_gain, w_out):
    rows_all, cols_all, width = xin.shape
    heads = rate.shape[1]
    head = width // heads
    half = heads // 2
    proj = jnp.dot(xin.reshape(-1, width), w_proj, preferred_element_type=jnp.float32).reshape(rows_all, cols_all, -1)

    def one_head(number):
        values = lax.dynamic_slice_in_dim(xin, number * head, head, 2).astype(jnp.float32)
        result = jnp.zeros(values.shape, jnp.float32)
        for direction in range(4):
            base = direction * 2 * heads
            step_size = jax.nn.softplus(lax.dynamic_index_in_dim(proj, base + number, 2, keepdims=False))
            input_coef = lax.dynamic_index_in_dim(proj, base + heads + number // 2, 2, keepdims=False)
            output_coef = lax.dynamic_index_in_dim(proj, base + heads + half + number // 2, 2, keepdims=False)
            decay = jnp.exp(-rate[direction][number] * step_size)
            drive = (step_size * input_coef)[..., None] * values
            backward = direction % 2 == 1
            if direction < 2:
                lines = scan_lines(jnp.swapaxes(decay, 0, 1), jnp.swapaxes(drive, 0, 1), jnp.swapaxes(output_coef, 0, 1), backward)
                result = result + jnp.swapaxes(lines, 0, 1)
            else:
                result = result + scan_lines(decay, drive, output_coef, backward)
        return result
    stacked = lax.map(one_head, jnp.arange(heads, dtype=jnp.int32))
    total = jnp.moveaxis(stacked, 0, 2).reshape(rows_all, cols_all, width) + skip * xin.astype(jnp.float32)
    scale = lax.rsqrt(lax.optimization_barrier(jnp.mean(total * total, axis=-1, keepdims=True)) + 1e-05)
    normed = (total * scale * norm_gain * jax.nn.silu(gate_in.astype(jnp.float32))).astype(jnp.bfloat16)
    mixed = jnp.dot(normed.reshape(-1, width), w_out, preferred_element_type=jnp.float32)
    return mixed.reshape(rows_all, cols_all, -1).astype(jnp.bfloat16)
```

```python
import functools

import jax
import jax.numpy as jnp
from jax import lax
from jax.experimental import pallas as pl
from jax.experimental.pallas import tpu as pltpu
from jax.sharding import PartitionSpec as P

MESH = pl.DeviceIdType.MESH
F32 = jnp.float32
BF16 = jnp.bfloat16

R, C, E, D, HEADS = 8, 64, 1024, 512, 16
PX = R * C
HALF = C // 2
LANES = 128
TILES = E // LANES
WIDE = E + LANES
NB = 256
CHUNKS = E // NB
ZERO_ROW = 112

NZ, NX, NCORE, NCOL = 4, 4, 2, 8

S_CORE, S_X, S_COLS, S_Z, S_BACK, S_LAST, N_SEM = 0, 1, 4, 11, 14, 17, 18


def split(v):
    hi = v.astype(BF16)
    lo = (v - hi.astype(F32)).astype(BF16)
    return jnp.concatenate([hi, lo], axis=-1)


def mxu(a, b):
    return jnp.dot(a, b, preferred_element_type=F32)


def kernel(x_hbm, g_hbm, wp_hbm, rate_ref, skip_ref, gain_ref, wo_hbm, o_hbm,
           xb, gb, wp, wo, ob, zsel, c1f, v_hl, d_hl, c1_hl, l_hl, h_hl, fv,
           x32, base, ro2, ro3, gg, hd0, hb0, ho0, hd1, hb1, ho1,
           s0, ee, tt, xe, px, gx, tz, ze, sc, rc, fxp, cc, pc, he, hr, nb,
           lsem, ssem, rsem):
    rows = lax.axis_index("rows")
    col = lax.axis_index("cols")
    core = rows % NCORE
    xi = (rows // NCORE) % NX
    zi = rows // (NCORE * NX)

    core_peer = {"rows": rows + 1 - 2 * core}
    x_dst = [(xi + d) % NX for d in range(1, NX)]
    x_peers = [{"rows": (zi * NX + t) * NCORE + core} for t in x_dst]
    z_peers = [{"rows": (((zi + d) % NZ) * NX + xi) * NCORE + core} for d in range(1, NZ)]
    c_peers = [{"cols": (col + d) % NCOL} for d in range(1, NCOL)]
    peers = [core_peer] + x_peers + z_peers + c_peers

    barrier = pltpu.get_barrier_semaphore()
    for peer in peers:
        pl.semaphore_signal(barrier, inc=1, device_id=peer, device_id_type=MESH)

    load_wp = pltpu.make_async_copy(wp_hbm, wp, lsem.at[0])
    load_x = pltpu.make_async_copy(x_hbm, xb, lsem.at[1])
    load_g = pltpu.make_async_copy(g_hbm, gb, lsem.at[2])
    load_wo = pltpu.make_async_copy(wo_hbm, wo, lsem.at[3])
    load_wp.start()
    load_x.start()
    load_g.start()
    load_wo.start()

    def remote(src, dst, number, peer):
        return pltpu.make_async_remote_copy(
            src_ref=src, dst_ref=dst, send_sem=ssem.at[number], recv_sem=rsem.at[number],
            device_id=peer, device_id_type=MESH)

    zsel[...] = jnp.zeros_like(zsel)
    head_row = lax.broadcasted_iota(jnp.int32, (HEADS, E), 0)
    head_col = lax.broadcasted_iota(jnp.int32, (HEADS, E), 1) // (E // HEADS)
    zsel[ZERO_ROW:ZERO_ROW + HEADS, :] = (head_row == head_col).astype(F32).astype(BF16)

    def sel(off, cols):
        part = zsel[ZERO_ROW - off:ZERO_ROW - off + LANES, cols]
        return jnp.concatenate([part, part], axis=0)

    def chunk(n):
        return pl.ds(pl.multiple_of(n * NB, NB), NB)

    def spread(v, off):
        return mxu(split(v), sel(off, slice(0, E)))

    src_lane = lax.broadcasted_iota(jnp.int32, (LANES, 2 * LANES), 0)
    lane = lax.broadcasted_iota(jnp.int32, (LANES, 2 * LANES), 1)
    within = lane % 64
    h = within % 16
    want = 32 * (within // 16) + jnp.where(lane < 128, h, jnp.where(lane < 192, 16 + h // 2, 24 + h // 2))
    pick = (src_lane == want).astype(F32).astype(BF16)
    rate = rate_ref[...]
    rate_lane = jnp.concatenate([rate[k:k + 1, :] for k in range(4)] * 2, axis=1)
    load_wp.wait()
    w2 = mxu(wp[...], pick).astype(BF16)
    load_x.wait()
    proj = mxu(xb[...].reshape(PX, E), w2)
    pre = proj[:, :LANES]
    coef = proj[:, LANES:]
    step = jnp.maximum(pre, 0.0) + jnp.log1p(jnp.exp(-jnp.abs(pre)))
    logd = -rate_lane * step
    lane1 = lax.broadcasted_iota(jnp.int32, (PX, LANES), 1)
    c1 = jnp.where(lane1 < 64, step * coef, coef)
    c1f[...] = c1
    l_hl[...] = split(logd)
    d_hl[...] = split(jnp.exp(logd))
    c1_hl[...] = split(c1)

    logr = [logd[r * C:(r + 1) * C, :] for r in range(R)]
    up = [logr[0]]
    for r in range(1, R):
        up.append(up[-1] + logr[r])
    down = [logr[R - 1]]
    for r in range(R - 2, -1, -1):
        down.insert(0, down[0] + logr[r])
    zero = jnp.zeros((C, LANES), F32)
    lane2 = lax.broadcasted_iota(jnp.int32, (C, LANES), 1)
    falling = (lane2 % 64) >= 48
    for r in range(R):
        before = up[r - 1] if r else zero
        after = down[r + 1] if r < R - 1 else zero
        tail = jnp.where(falling, before, after)
        reach = jnp.where(falling, down[r], up[r])
        v = jnp.exp(jnp.where(lane2 < 64, tail, reach)) * c1[r * C:(r + 1) * C, :]
        v_hl[r] = split(v)
    fv[...] = jnp.exp(up[R - 1])

    def column_ends(start, dst):
        lhs = v_hl[:, pl.ds(start, HALF), :].reshape(R * HALF, 2 * LANES)
        for n in range(CHUNKS):
            cs = slice(n * NB, (n + 1) * NB)
            xh = [xb[r, pl.ds(start, HALF), cs].astype(F32) for r in range(R)]
            for i in range(2):
                w = mxu(lhs, sel(32 + 16 * i, cs))
                acc = w[:HALF] * xh[0]
                for r in range(1, R):
                    acc = acc + w[r * HALF:(r + 1) * HALF] * xh[r]
                dst[i, :, cs] = acc
        for i in range(2):
            dst[i, :, E:] = fv[pl.ds(start, HALF), :]

    own = pl.multiple_of(core * HALF, HALF)
    other = pl.multiple_of((1 - core) * HALF, HALF)
    column_ends(other, s0)
    pl.semaphore_wait(barrier, len(peers))
    to_core = remote(s0, ee.at[core], S_CORE, core_peer)
    to_core.start()
    column_ends(own, ee.at[core])

    to_core.wait_recv()
    for i in range(2):
        first, second = ee.at[i, i], ee.at[1 - i, i]
        t = second[:, :E] + spread(second[:, E:], 32 + 16 * i) * first[:, :E]
        f = second[:, E:] * first[:, E:]
        for q in range(NX):
            tt[q, i, :, :E] = t[q * 8:(q + 1) * 8]
            tt[q, i, :, E:] = f[q * 8:(q + 1) * 8]
    to_x = [remote(tt.at[x_dst[d]], xe.at[xi], S_X + d, x_peers[d]) for d in range(NX - 1)]
    for copy in to_x:
        copy.start()
    xe[xi] = tt[xi]

    bt = lax.broadcasted_iota(jnp.int32, (256, 256), 0)
    bs = lax.broadcasted_iota(jnp.int32, (256, 256), 1)
    same = (bt // C) == (bs // C)
    behind = (same & (bs > bt)).astype(F32).astype(BF16)
    ahead = (same & (bs < bt)).astype(F32).astype(BF16)
    lane3 = lax.broadcasted_iota(jnp.int32, (256, LANES), 1)
    for m in range(PX // 256):
        ps = slice(m * 256, (m + 1) * 256)
        lh = l_hl[ps, :]
        a = mxu(behind, lh)
        b = mxu(ahead, lh)
        cum = jnp.where(lane3 < 16, a[:, :LANES] + a[:, LANES:], b[:, :LANES] + b[:, LANES:])
        h_hl[ps, :] = split(jnp.exp(cum) * c1f[ps, :])
    row_of = lax.broadcasted_iota(jnp.int32, (R, PX), 1) // C
    whole = (row_of == lax.broadcasted_iota(jnp.int32, (R, PX), 0)).astype(F32).astype(BF16)
    ft = mxu(whole, l_hl[...])
    ft = jnp.exp(ft[:, :LANES] + ft[:, LANES:])

    def row_ends(n, _):
        cs = chunk(n)
        for i in range(2):
            w = mxu(h_hl[...], sel(16 * i, cs)).reshape(R, C, NB)
            he[i, :, cs] = jnp.sum(w * xb[:, :, cs].astype(F32), axis=1)
        return 0

    lax.fori_loop(0, CHUNKS, row_ends, 0)
    for i in range(2):
        he[i, :, E:] = ft
    to_cols = [remote(he.at[(col + d) // NCOL], hr.at[col], S_COLS + d - 1, c_peers[d - 1])
               for d in range(1, NCOL)]
    for copy in to_cols:
        copy.start()
    hr[col] = he[0]

    def column_scans(n, _):
        cs = chunk(n)
        xs = [xb[r, :, cs].astype(F32) for r in range(R)]
        sk = skip_ref[:, cs]
        acc = [sk * xs[r] for r in range(R)]
        for r in range(R):
            for t in range(2):
                x32[2 * n + t, r * C:(r + 1) * C, :] = xs[r][:, t * LANES:(t + 1) * LANES]
        for i in range(2):
            off = 32 + 16 * i
            dd = mxu(d_hl[...], sel(off, cs))
            bb = mxu(c1_hl[...], sel(off, cs))
            oo = mxu(c1_hl[...], sel(64 + off, cs))
            state = None
            for r in (range(R) if i == 0 else range(R - 1, -1, -1)):
                ps = slice(r * C, (r + 1) * C)
                push = bb[ps] * xs[r]
                state = push if state is None else dd[ps] * state + push
                acc[r] = acc[r] + oo[ps] * state
        for r in range(R):
            for t in range(2):
                base[2 * n + t, r * C:(r + 1) * C, :] = acc[r][:, t * LANES:(t + 1) * LANES]
        return 0

    lax.fori_loop(0, CHUNKS, column_scans, 0)

    def spread_all(n, _):
        cs = chunk(n)
        dv = d_hl[...]
        cv = c1_hl[...]
        vv = v_hl[...].reshape(PX, 2 * LANES)
        for lhs, off, dst in ((dv, 0, hd0), (cv, 0, hb0), (cv, 64, ho0), (dv, 16, hd1), (cv, 16, hb1),
                              (cv, 80, ho1), (vv, 96, ro2), (vv, 112, ro3)):
            w = mxu(lhs, sel(off, cs))
            for t in range(2):
                dst[2 * n + t] = w[:, t * LANES:(t + 1) * LANES]
        return 0

    lax.fori_loop(0, CHUNKS, spread_all, 0)
    load_g.wait()

    def gates(n, _):
        cs = chunk(n)
        gain = gain_ref[:, cs]
        for r in range(R):
            g = gb[r, :, cs].astype(F32)
            w = gain * (g / (1.0 + jnp.exp(-g)))
            for t in range(2):
                gg[2 * n + t, r * C:(r + 1) * C, :] = w[:, t * LANES:(t + 1) * LANES]
        return 0

    lax.fori_loop(0, CHUNKS, gates, 0)

    for i in range(2):
        fxp[i] = spread(ee[i, i, :, E:], 32 + 16 * i)

    for copy in to_x:
        copy.wait_recv()
    fc = xe[0, 0, :, E:]
    for q in range(1, NX):
        fc = fc * xe[q, 0, :, E:]
    for i in range(2):
        fs = spread(xe[:, i, :, E:].reshape(NX * 8, LANES), 32 + 16 * i)
        acc = jnp.zeros((8, E), F32)
        g = jnp.ones((8, E), F32)
        for q in (range(NX) if i == 0 else range(NX - 1, -1, -1)):
            f = fs[q * 8:(q + 1) * 8]
            px[q, i] = acc
            gx[q, i] = g
            acc = xe[q, i, :, :E] + f * acc
            g = g * f
        tz[i, :, :E] = acc
        tz[i, :, E:] = fc
    to_z = [remote(tz.at[(zi + d) // NZ], ze.at[zi], S_Z + d - 1, z_peers[d - 1]) for d in range(1, NZ)]
    for copy in to_z:
        copy.start()
    ze[zi] = tz[0]

    for copy in to_cols:
        copy.wait_recv()
    fh = hr[:, :, E:].reshape(NCOL * R, LANES)
    f0 = spread(fh, 0)
    f1 = spread(fh, 16)
    in0 = jnp.zeros((R, E), F32)
    in1 = jnp.zeros((R, E), F32)
    for j in range(NCOL):
        in0 = jnp.where(j < col, hr[j, :, :E] + f0[j * R:(j + 1) * R] * in0, in0)
    for j in range(NCOL - 1, -1, -1):
        in1 = jnp.where(j > col, hr[j, :, :E] + f1[j * R:(j + 1) * R] * in1, in1)

    def row_step(c, states):
        out = []
        for at, hd, hb, ho, first in ((c, hd0, hb0, ho0, 0), (C - 1 - c, hd1, hb1, ho1, TILES)):
            ps = pl.ds(at, R, stride=C)
            for t in range(TILES):
                s = hd[t, ps, :] * states[first + t] + hb[t, ps, :] * x32[t, ps, :]
                base[t, ps, :] = base[t, ps, :] + ho[t, ps, :] * s
                out.append(s)
        return tuple(out)

    start = [in0[:, t * LANES:(t + 1) * LANES] for t in range(TILES)]
    start += [in1[:, t * LANES:(t + 1) * LANES] for t in range(TILES)]
    lax.fori_loop(0, C, row_step, tuple(start))
    load_wo.wait()

    for copy in to_z:
        copy.wait_recv()
    fz = ze[:, :, E:].reshape(NZ * 8, LANES)
    for i in range(2):
        fs = spread(fz, 32 + 16 * i)
        acc = jnp.zeros((8, E), F32)
        for j in (range(NZ) if i == 0 else range(NZ - 1, -1, -1)):
            use = (j < zi) if i == 0 else (j > zi)
            acc = jnp.where(use, ze[j, :, :E] + fs[j * 8:(j + 1) * 8] * acc, acc)
        for q in range(NX):
            sc[q, i] = px[q, i] + gx[q, i] * acc
    to_back = [remote(sc.at[x_dst[d]], rc.at[xi], S_BACK + d, x_peers[d]) for d in range(NX - 1)]
    for copy in to_back:
        copy.start()
    rc[xi] = sc[xi]
    for copy in to_back:
        copy.wait_recv()

    for i in range(2):
        for q in range(NX):
            qs = slice(q * 8, (q + 1) * 8)
            carry = rc[q, i]
            cc[i, i, qs, :] = carry
            cc[1 - i, i, qs, :] = ee[i, i, qs, :E] + fxp[i, qs, :] * carry
    to_last = remote(cc.at[1 - core], pc, S_LAST, core_peer)
    to_last.start()

    def finish(start, carry, number):
        def line(r, _):
            ps = pl.ds(pl.multiple_of(r * C + start, HALF), HALF)
            tot = []
            sq = jnp.zeros((HALF, LANES), F32)
            for t in range(TILES):
                ls = slice(t * LANES, (t + 1) * LANES)
                v = base[t, ps, :] + ro2[t, ps, :] * carry[0, :, ls] + ro3[t, ps, :] * carry[1, :, ls]
                sq = sq + v * v
                tot.append(v)
            scale = lax.rsqrt(jnp.sum(sq, axis=-1, keepdims=True) * (1.0 / E) + 1e-05)
            for t in range(TILES):
                ls = slice(t * LANES, (t + 1) * LANES)
                nb[r, :, ls] = (tot[t] * scale * gg[t, ps, :]).astype(BF16)
            return 0

        lax.fori_loop(0, R, line, 0)
        res = mxu(nb[...].reshape(R * HALF, E), wo[...])
        ob[:, pl.ds(start, HALF), :] = res.astype(BF16).reshape(R, HALF, D)
        copy = pltpu.make_async_copy(ob.at[:, pl.ds(start, HALF), :], o_hbm.at[:, pl.ds(start, HALF), :], lsem.at[number])
        copy.start()
        return copy

    out_own = finish(own, cc.at[core], 4)
    to_last.wait_recv()
    out_other = finish(other, pc, 5)
    for copy in [to_core, to_last] + to_x + to_cols + to_z + to_back:
        copy.wait_send()
    out_own.wait()
    out_other.wait()


def local(xin, gate_in, w_proj, rate, skip, norm_gain, w_out):
    vmem = pl.BlockSpec(memory_space=pltpu.VMEM)
    hbm = pl.BlockSpec(memory_space=pl.ANY)
    big = pltpu.VMEM((TILES, PX, LANES), F32)
    compact = pltpu.VMEM((PX, 2 * LANES), BF16)
    scratch = [
        pltpu.VMEM((R, C, E), BF16),
        pltpu.VMEM((R, C, E), BF16),
        pltpu.VMEM((E, LANES), BF16),
        pltpu.VMEM((E, D), BF16),
        pltpu.VMEM((R, C, D), BF16),
        pltpu.VMEM((ZERO_ROW + LANES, E), BF16),
        pltpu.VMEM((PX, LANES), F32),
        pltpu.VMEM((R, C, 2 * LANES), BF16),
        compact, compact, compact, compact,
        pltpu.VMEM((C, LANES), F32),
        big, big, big, big, big, big, big, big, big, big, big,
        pltpu.VMEM((2, HALF, WIDE), F32),
        pltpu.VMEM((2, 2, HALF, WIDE), F32),
        pltpu.VMEM((NX, 2, 8, WIDE), F32),
        pltpu.VMEM((NX, 2, 8, WIDE), F32),
        pltpu.VMEM((NX, 2, 8, E), F32),
        pltpu.VMEM((NX, 2, 8, E), F32),
        pltpu.VMEM((2, 8, WIDE), F32),
        pltpu.VMEM((NZ, 8, WIDE), F32),
        pltpu.VMEM((NX, 2, 8, E), F32),
        pltpu.VMEM((NX, 2, 8, E), F32),
        pltpu.VMEM((2, HALF, E), F32),
        pltpu.VMEM((2, 2, HALF, E), F32),
        pltpu.VMEM((2, HALF, E), F32),
        pltpu.VMEM((2, R, WIDE), F32),
        pltpu.VMEM((NCOL, R, WIDE), F32),
        pltpu.VMEM((R, HALF, E), BF16),
        pltpu.SemaphoreType.DMA((6,)),
        pltpu.SemaphoreType.DMA((N_SEM,)),
        pltpu.SemaphoreType.DMA((N_SEM,)),
    ]
    return pl.pallas_call(
        kernel,
        out_shape=jax.ShapeDtypeStruct((R, C, D), BF16),
        in_specs=[hbm, hbm, hbm, vmem, vmem, vmem, hbm],
        out_specs=hbm,
        scratch_shapes=scratch,
        compiler_params=pltpu.CompilerParams(
            collective_id=0, has_side_effects=True, vmem_limit_bytes=60 * 1024 * 1024),
    )(xin, gate_in, w_proj, rate, skip.reshape(1, E), norm_gain.reshape(1, E), w_out)


def solution(mesh):
    in_specs = (P("rows", "cols", None), P("rows", "cols", None), P(), P(), P(), P(), P())
    return jax.shard_map(local, mesh=mesh, in_specs=in_specs, out_specs=P("rows", "cols", None), check_vma=False)
```

```python
import functools

import jax
import jax.numpy as jnp
from jax import lax
from jax.experimental import pallas as pl
from jax.experimental.pallas import tpu as pltpu
from jax.sharding import PartitionSpec as P

MESH = pl.DeviceIdType.MESH
F32 = jnp.float32
BF16 = jnp.bfloat16

R, C, E, D, HEADS = 8, 64, 1024, 512, 16
PX = R * C
HALF = C // 2
LANES = 128
TILES = E // LANES
WIDE = E + LANES
NB = 256
CHUNKS = E // NB
ZERO_ROW = 112
RS = 72

NZ, NX, NCORE, NCOL = 4, 4, 2, 8

S_CORE, S_X, S_COLS, S_Z, S_BACK, S_LAST, N_SEM = 0, 2, 8, 15, 18, 24, 26


def split(v):
    hi = v.astype(BF16)
    lo = (v - hi.astype(F32)).astype(BF16)
    return jnp.concatenate([hi, lo], axis=-1)


def mxu(a, b):
    return jnp.dot(a, b, preferred_element_type=F32)


def kernel(x_hbm, g_hbm, wp_hbm, rate_ref, skip_ref, gain_ref, wo_hbm, o_hbm,
           xb, gb, wp, wo, ob, zsel, c1f, v_hl, d_hl, c1_hl, l_hl, h_hl, fv,
           base, ro2, ro3, gg, hd0, hb0, ho0, hd1, hb1, ho1,
           s0, ee, tt, xe, px, gx, tz, ze, sc, rc, fxp, cc, pc, he, hr, nb,
           lsem, ssem, rsem):
    rows = lax.axis_index("rows")
    col = lax.axis_index("cols")
    core = rows % NCORE
    xi = (rows // NCORE) % NX
    zi = rows // (NCORE * NX)

    core_peer = {"rows": rows + 1 - 2 * core}
    x_dst = [(xi + d) % NX for d in range(1, NX)]
    x_peers = [{"rows": (zi * NX + t) * NCORE + core} for t in x_dst]
    z_peers = [{"rows": (((zi + d) % NZ) * NX + xi) * NCORE + core} for d in range(1, NZ)]
    c_peers = [{"cols": (col + d) % NCOL} for d in range(1, NCOL)]
    peers = [core_peer] + x_peers + z_peers + c_peers

    barrier = pltpu.get_barrier_semaphore()
    for peer in peers:
        pl.semaphore_signal(barrier, inc=1, device_id=peer, device_id_type=MESH)

    load_wp = pltpu.make_async_copy(wp_hbm, wp, lsem.at[0])
    load_x = pltpu.make_async_copy(x_hbm, xb, lsem.at[1])
    load_g = pltpu.make_async_copy(g_hbm, gb, lsem.at[2])
    load_wo = pltpu.make_async_copy(wo_hbm, wo, lsem.at[3])
    load_wp.start()
    load_x.start()
    load_g.start()
    load_wo.start()

    def remote(src, dst, number, peer):
        return pltpu.make_async_remote_copy(
            src_ref=src, dst_ref=dst, send_sem=ssem.at[number], recv_sem=rsem.at[number],
            device_id=peer, device_id_type=MESH)

    zsel[...] = jnp.zeros_like(zsel)
    head_row = lax.broadcasted_iota(jnp.int32, (HEADS, E), 0)
    head_col = lax.broadcasted_iota(jnp.int32, (HEADS, E), 1) // (E // HEADS)
    zsel[ZERO_ROW:ZERO_ROW + HEADS, :] = (head_row == head_col).astype(F32).astype(BF16)

    def sel(off, cols):
        part = zsel[ZERO_ROW - off:ZERO_ROW - off + LANES, cols]
        return jnp.concatenate([part, part], axis=0)

    def chunk(n):
        return pl.ds(pl.multiple_of(n * NB, NB), NB)

    def spread(v, off):
        return mxu(split(v), sel(off, slice(0, E)))

    src_lane = lax.broadcasted_iota(jnp.int32, (LANES, 2 * LANES), 0)
    lane = lax.broadcasted_iota(jnp.int32, (LANES, 2 * LANES), 1)
    within = lane % 64
    h = within % 16
    want = 32 * (within // 16) + jnp.where(lane < 128, h, jnp.where(lane < 192, 16 + h // 2, 24 + h // 2))
    pick = (src_lane == want).astype(F32).astype(BF16)
    rate = rate_ref[...]
    rate_lane = jnp.concatenate([rate[k:k + 1, :] for k in range(4)] * 2, axis=1)
    load_wp.wait()
    w2 = mxu(wp[...], pick).astype(BF16)
    load_x.wait()
    proj = mxu(xb[...].reshape(PX, E), w2)
    pre = proj[:, :LANES]
    coef = proj[:, LANES:]
    step = jnp.maximum(pre, 0.0) + jnp.log1p(jnp.exp(-jnp.abs(pre)))
    logd = -rate_lane * step
    lane1 = lax.broadcasted_iota(jnp.int32, (PX, LANES), 1)
    c1 = jnp.where(lane1 < 64, step * coef, coef)
    c1f[...] = c1
    l_hl[...] = split(logd)
    d_hl[...] = split(jnp.exp(logd))
    c1_hl[...] = split(c1)

    logr = [logd[r * C:(r + 1) * C, :] for r in range(R)]
    up = [logr[0]]
    for r in range(1, R):
        up.append(up[-1] + logr[r])
    down = [logr[R - 1]]
    for r in range(R - 2, -1, -1):
        down.insert(0, down[0] + logr[r])
    zero = jnp.zeros((C, LANES), F32)
    lane2 = lax.broadcasted_iota(jnp.int32, (C, LANES), 1)
    falling = (lane2 % 64) >= 48
    for r in range(R):
        before = up[r - 1] if r else zero
        after = down[r + 1] if r < R - 1 else zero
        tail = jnp.where(falling, before, after)
        reach = jnp.where(falling, down[r], up[r])
        v = jnp.exp(jnp.where(lane2 < 64, tail, reach)) * c1[r * C:(r + 1) * C, :]
        v_hl[r] = split(v)
    fv[...] = jnp.exp(up[R - 1])

    def column_ends(start, i, dst):
        lhs = v_hl[:, pl.ds(start, HALF), :].reshape(R * HALF, 2 * LANES)
        for n in range(CHUNKS):
            cs = slice(n * NB, (n + 1) * NB)
            w = mxu(lhs, sel(32 + 16 * i, cs))
            acc = w[:HALF] * xb[0, pl.ds(start, HALF), cs].astype(F32)
            for r in range(1, R):
                acc = acc + w[r * HALF:(r + 1) * HALF] * xb[r, pl.ds(start, HALF), cs].astype(F32)
            dst[i, :, cs] = acc
        dst[i, :, E:] = fv[pl.ds(start, HALF), :]

    own = pl.multiple_of(core * HALF, HALF)
    other = pl.multiple_of((1 - core) * HALF, HALF)
    to_core = [remote(s0.at[i], ee.at[core, i], S_CORE + i, core_peer) for i in range(2)]
    column_ends(other, 1, s0)
    pl.semaphore_wait(barrier, len(peers))
    to_core[1].start()
    column_ends(other, 0, s0)
    to_core[0].start()
    column_ends(own, 1, ee.at[core])
    column_ends(own, 0, ee.at[core])

    to_x = [[remote(tt.at[x_dst[d], i], xe.at[xi, i], S_X + 3 * i + d, x_peers[d]) for d in range(NX - 1)]
            for i in range(2)]
    for i in (1, 0):
        to_core[i].wait_recv()
        first, second = ee.at[i, i], ee.at[1 - i, i]
        t = second[:, :E] + spread(second[:, E:], 32 + 16 * i) * first[:, :E]
        f = second[:, E:] * first[:, E:]
        for q in range(NX):
            tt[q, i, :, :E] = t[q * 8:(q + 1) * 8]
            tt[q, i, :, E:] = f[q * 8:(q + 1) * 8]
        for copy in to_x[i]:
            copy.start()
    xe[xi] = tt[xi]

    bt = lax.broadcasted_iota(jnp.int32, (256, 256), 0)
    bs = lax.broadcasted_iota(jnp.int32, (256, 256), 1)
    same = (bt // C) == (bs // C)
    behind = (same & (bs > bt)).astype(F32).astype(BF16)
    ahead = (same & (bs < bt)).astype(F32).astype(BF16)
    lane3 = lax.broadcasted_iota(jnp.int32, (256, LANES), 1)
    for m in range(PX // 256):
        ps = slice(m * 256, (m + 1) * 256)
        lh = l_hl[ps, :]
        a = mxu(behind, lh)
        b = mxu(ahead, lh)
        cum = jnp.where(lane3 < 16, a[:, :LANES] + a[:, LANES:], b[:, :LANES] + b[:, LANES:])
        h_hl[ps, :] = split(jnp.exp(cum) * c1f[ps, :])
    row_of = lax.broadcasted_iota(jnp.int32, (R, PX), 1) // C
    whole = (row_of == lax.broadcasted_iota(jnp.int32, (R, PX), 0)).astype(F32).astype(BF16)
    ft = mxu(whole, l_hl[...])
    ft = jnp.exp(ft[:, :LANES] + ft[:, LANES:])

    def row_ends(n, _):
        cs = chunk(n)
        for i in range(2):
            w = mxu(h_hl[...], sel(16 * i, cs)).reshape(R, C, NB)
            he[i, :, cs] = jnp.sum(w * xb[:, :, cs].astype(F32), axis=1)
        return 0

    lax.fori_loop(0, CHUNKS, row_ends, 0)
    for i in range(2):
        he[i, :, E:] = ft
    to_cols = [remote(he.at[(col + d) // NCOL], hr.at[col], S_COLS + d - 1, c_peers[d - 1])
               for d in range(1, NCOL)]
    for copy in to_cols:
        copy.start()
    hr[col] = he[0]

    def column_scans(n, _):
        cs = chunk(n)
        xs = [xb[r, :, cs].astype(F32) for r in range(R)]
        sk = skip_ref[:, cs]
        acc = [sk * xs[r] for r in range(R)]
        for i in range(2):
            off = 32 + 16 * i
            dd = mxu(d_hl[...], sel(off, cs))
            bb = mxu(c1_hl[...], sel(off, cs))
            oo = mxu(c1_hl[...], sel(64 + off, cs))
            state = None
            for r in (range(R) if i == 0 else range(R - 1, -1, -1)):
                ps = slice(r * C, (r + 1) * C)
                push = bb[ps] * xs[r]
                state = push if state is None else dd[ps] * state + push
                acc[r] = acc[r] + oo[ps] * state
        for r in range(R):
            for t in range(2):
                base[2 * n + t, r * RS:r * RS + C, :] = acc[r][:, t * LANES:(t + 1) * LANES]
        return 0

    lax.fori_loop(0, CHUNKS, column_scans, 0)

    to_z = [remote(tz.at[(zi + d) // NZ], ze.at[zi], S_Z + d - 1, z_peers[d - 1]) for d in range(1, NZ)]
    for i in (1, 0):
        for copy in to_x[i]:
            copy.wait_recv()
        fc = xe[0, i, :, E:]
        for q in range(1, NX):
            fc = fc * xe[q, i, :, E:]
        fs = spread(xe[:, i, :, E:].reshape(NX * 8, LANES), 32 + 16 * i)
        acc = jnp.zeros((8, E), F32)
        g = jnp.ones((8, E), F32)
        for q in (range(NX) if i == 0 else range(NX - 1, -1, -1)):
            f = fs[q * 8:(q + 1) * 8]
            px[i, q] = acc
            gx[i, q] = g
            acc = xe[q, i, :, :E] + f * acc
            g = g * f
        tz[i, :, :E] = acc
        tz[i, :, E:] = fc
        for d in range(1, NZ):
            @pl.when((zi + d) // NZ == i)
            def _():
                to_z[d - 1].start()
    ze[zi] = tz[0]

    for i in range(2):
        fxp[i] = spread(ee[i, i, :, E:], 32 + 16 * i)

    def back_copies(i, order):
        return [remote(sc.at[i, x_dst[d]], rc.at[i, xi], S_BACK + 3 * order + d, x_peers[d]) for d in range(NX - 1)]

    def over_groups(i, order):
        for d in range(1, NZ):
            @pl.when(1 - (zi + NZ - d) // NZ == i)
            def _():
                to_z[d - 1].wait_recv()
        before = zi + i * (NZ - 1 - 2 * zi)
        slots = []
        for m in range(NZ - 1):
            valid = (before + NZ - 1 - m) // NZ
            slots.append(valid * (m + i * (NZ - 1 - 2 * m)) + (1 - valid) * zi)
        at = pl.multiple_of(ZERO_ROW - 32 - 16 * i, 16)
        part = zsel[pl.ds(at, LANES), :]
        lhs = jnp.concatenate([ze[j, :, E:] for j in slots], axis=0)
        fs = mxu(split(lhs), jnp.concatenate([part, part], axis=0))
        acc = jnp.zeros((8, E), F32)
        for m, j in enumerate(slots):
            acc = jnp.where(m < before, ze[j, :, :E] + fs[m * 8:(m + 1) * 8] * acc, acc)
        for q in range(NX):
            sc[i, q] = px[i, q] + gx[i, q] * acc
        for copy in back_copies(i, order):
            copy.start()
        rc[i, xi] = sc[i, xi]

    def to_last(i, order):
        return remote(cc.at[1 - core, i], pc.at[i], S_LAST + order, core_peer)

    def over_chip(i, order):
        for copy in back_copies(i, order):
            copy.wait_recv()
        carry = rc[i].reshape(HALF, E)
        cc[i, i] = carry
        cc[1 - i, i] = ee[i, i, :, :E] + fxp[i] * carry
        to_last(i, order).start()

    near = zi // (NZ // 2)
    far = 1 - near
    over_groups(near, 0)

    def row_spread(n, _):
        cs = chunk(n)
        dv = d_hl[...]
        cv = c1_hl[...]
        xs = xb[:, :, cs].astype(F32)
        for lhs, off, drive, dst in ((dv, 0, 0, hd0), (cv, 0, 1, hb0), (cv, 64, 0, ho0),
                                     (dv, 16, 0, hd1), (cv, 16, 1, hb1), (cv, 80, 0, ho1)):
            w = mxu(lhs, sel(off, cs)).reshape(R, C, NB)
            if drive:
                w = w * xs
            for r in range(R):
                for t in range(2):
                    dst[2 * n + t, r * RS:r * RS + C, :] = w[r, :, t * LANES:(t + 1) * LANES]
        return 0

    lax.fori_loop(0, CHUNKS, row_spread, 0)
    for copy in to_cols:
        copy.wait_recv()
    fh = hr[:, :, E:].reshape(NCOL * R, LANES)
    f0 = spread(fh, 0)
    f1 = spread(fh, 16)
    in0 = jnp.zeros((R, E), F32)
    in1 = jnp.zeros((R, E), F32)
    for j in range(NCOL):
        in0 = jnp.where(j < col, hr[j, :, :E] + f0[j * R:(j + 1) * R] * in0, in0)
    for j in range(NCOL - 1, -1, -1):
        in1 = jnp.where(j > col, hr[j, :, :E] + f1[j * R:(j + 1) * R] * in1, in1)

    def row_step(c, states):
        out = []
        for at, hd, hb, ho, first in ((c, hd0, hb0, ho0, 0), (C - 1 - c, hd1, hb1, ho1, TILES)):
            ps = pl.ds(at, R, stride=RS)
            for t in range(TILES):
                s = hd[t, ps, :] * states[first + t] + hb[t, ps, :]
                base[t, ps, :] = base[t, ps, :] + ho[t, ps, :] * s
                out.append(s)
        return tuple(out)

    begin = [in0[:, t * LANES:(t + 1) * LANES] for t in range(TILES)]
    begin += [in1[:, t * LANES:(t + 1) * LANES] for t in range(TILES)]
    lax.fori_loop(0, C, row_step, tuple(begin))

    over_chip(near, 0)
    over_groups(far, 1)

    load_g.wait()
    load_wo.wait()

    def tail_spread(n, _):
        cs = chunk(n)
        gain = gain_ref[:, cs]
        vv = v_hl[...].reshape(PX, 2 * LANES)
        for off, dst in ((96, ro2), (112, ro3)):
            w = mxu(vv, sel(off, cs))
            for r in range(R):
                for t in range(2):
                    dst[2 * n + t, r * RS:r * RS + C, :] = w[r * C:(r + 1) * C, t * LANES:(t + 1) * LANES]
        for r in range(R):
            g = gb[r, :, cs].astype(F32)
            w = gain * (g / (1.0 + jnp.exp(-g)))
            for t in range(2):
                gg[2 * n + t, r * RS:r * RS + C, :] = w[:, t * LANES:(t + 1) * LANES]
        return 0

    lax.fori_loop(0, CHUNKS, tail_spread, 0)
    over_chip(far, 1)

    def finish(start, carry, number):
        for part in range(2):
            for r in range(part * R // 2, (part + 1) * R // 2):
                ps = pl.ds(pl.multiple_of(r * RS + start, 8), HALF)
                tot = []
                sq = jnp.zeros((HALF, LANES), F32)
                for t in range(TILES):
                    ls = slice(t * LANES, (t + 1) * LANES)
                    v = base[t, ps, :] + ro2[t, ps, :] * carry[0, :, ls] + ro3[t, ps, :] * carry[1, :, ls]
                    sq = sq + v * v
                    tot.append(v)
                scale = lax.rsqrt(jnp.sum(sq, axis=-1, keepdims=True) * (1.0 / E) + 1e-05)
                for t in range(TILES):
                    ls = slice(t * LANES, (t + 1) * LANES)
                    nb[r, :, ls] = (tot[t] * scale * gg[t, ps, :]).astype(BF16)
            rs = slice(part * R // 2, (part + 1) * R // 2)
            res = mxu(nb[rs].reshape(R // 2 * HALF, E), wo[...])
            ob[rs, pl.ds(start, HALF), :] = res.astype(BF16).reshape(R // 2, HALF, D)
        copy = pltpu.make_async_copy(ob.at[:, pl.ds(start, HALF), :], o_hbm.at[:, pl.ds(start, HALF), :], lsem.at[number])
        copy.start()
        return copy

    out_own = finish(own, cc.at[core], 4)
    for order, i in ((0, near), (1, far)):
        to_last(i, order).wait_recv()
    out_other = finish(other, pc, 5)
    for copy in to_core + to_x[0] + to_x[1] + to_cols + to_z + back_copies(near, 0) + back_copies(far, 1):
        copy.wait_send()
    to_last(near, 0).wait_send()
    to_last(far, 1).wait_send()
    out_own.wait()
    out_other.wait()


def local(xin, gate_in, w_proj, rate, skip, norm_gain, w_out):
    vmem = pl.BlockSpec(memory_space=pltpu.VMEM)
    hbm = pl.BlockSpec(memory_space=pl.ANY)
    big = pltpu.VMEM((TILES, R * RS, LANES), F32)
    compact = pltpu.VMEM((PX, 2 * LANES), BF16)
    scratch = [
        pltpu.VMEM((R, C, E), BF16),
        pltpu.VMEM((R, C, E), BF16),
        pltpu.VMEM((E, LANES), BF16),
        pltpu.VMEM((E, D), BF16),
        pltpu.VMEM((R, C, D), BF16),
        pltpu.VMEM((ZERO_ROW + LANES, E), BF16),
        pltpu.VMEM((PX, LANES), F32),
        pltpu.VMEM((R, C, 2 * LANES), BF16),
        compact, compact, compact, compact,
        pltpu.VMEM((C, LANES), F32),
        big, big, big, big, big, big, big, big, big, big,
        pltpu.VMEM((2, HALF, WIDE), F32),
        pltpu.VMEM((2, 2, HALF, WIDE), F32),
        pltpu.VMEM((NX, 2, 8, WIDE), F32),
        pltpu.VMEM((NX, 2, 8, WIDE), F32),
        pltpu.VMEM((2, NX, 8, E), F32),
        pltpu.VMEM((2, NX, 8, E), F32),
        pltpu.VMEM((2, 8, WIDE), F32),
        pltpu.VMEM((NZ, 8, WIDE), F32),
        pltpu.VMEM((2, NX, 8, E), F32),
        pltpu.VMEM((2, NX, 8, E), F32),
        pltpu.VMEM((2, HALF, E), F32),
        pltpu.VMEM((2, 2, HALF, E), F32),
        pltpu.VMEM((2, HALF, E), F32),
        pltpu.VMEM((2, R, WIDE), F32),
        pltpu.VMEM((NCOL, R, WIDE), F32),
        pltpu.VMEM((R, HALF, E), BF16),
        pltpu.SemaphoreType.DMA((6,)),
        pltpu.SemaphoreType.DMA((N_SEM,)),
        pltpu.SemaphoreType.DMA((N_SEM,)),
    ]
    return pl.pallas_call(
        kernel,
        out_shape=jax.ShapeDtypeStruct((R, C, D), BF16),
        in_specs=[hbm, hbm, hbm, vmem, vmem, vmem, hbm],
        out_specs=hbm,
        scratch_shapes=scratch,
        compiler_params=pltpu.CompilerParams(
            collective_id=0, has_side_effects=True, vmem_limit_bytes=60 * 1024 * 1024),
    )(xin, gate_in, w_proj, rate, skip.reshape(1, E), norm_gain.reshape(1, E), w_out)


def solution(mesh):
    in_specs = (P("rows", "cols", None), P("rows", "cols", None), P(), P(), P(), P(), P())
    return jax.shard_map(local, mesh=mesh, in_specs=in_specs, out_specs=P("rows", "cols", None), check_vma=False)
```

```python
import functools

import jax
import jax.numpy as jnp
from jax import lax
from jax.experimental import pallas as pl
from jax.experimental.pallas import tpu as pltpu
from jax.sharding import PartitionSpec as P

MESH = pl.DeviceIdType.MESH
F32 = jnp.float32
BF16 = jnp.bfloat16

R, C, E, D, HEADS = 8, 64, 1024, 512, 16
PX = R * C
HALF = C // 2
LANES = 128
TILES = E // LANES
WIDE = E + LANES
NB = 256
CHUNKS = E // NB
ZERO_ROW = 112
RS = 72

NZ, NX, NCORE, NCOL = 4, 4, 2, 8

S_CORE, S_X, S_COLS, S_Z, S_BACK, S_LAST, N_SEM = 0, 2, 8, 15, 18, 24, 26


def split(v):
    hi = v.astype(BF16)
    lo = (v - hi.astype(F32)).astype(BF16)
    return jnp.concatenate([hi, lo], axis=-1)


def mxu(a, b):
    return jnp.dot(a, b, preferred_element_type=F32)


def kernel(x_hbm, g_hbm, wp_hbm, rate_ref, skip_ref, gain_ref, wo_hbm, ob,
           xb, gb, wp, wo, zsel, c1f, v_hl, d_hl, c1_hl, l_hl, h_hl, fv,
           base, ro2, ro3, gg, hd0, hb0, ho0, hd1, hb1, ho1,
           s0, ee, tt, xe, px, gx, tz, ze, sc, rc, fxp, cc, pc, he, hr, nb,
           lsem, ssem, rsem):
    rows = lax.axis_index("rows")
    col = lax.axis_index("cols")
    core = rows % NCORE
    xi = (rows // NCORE) % NX
    zi = rows // (NCORE * NX)

    core_peer = {"rows": rows + 1 - 2 * core}
    x_dst = [(xi + d) % NX for d in range(1, NX)]
    x_peers = [{"rows": (zi * NX + t) * NCORE + core} for t in x_dst]
    z_peers = [{"rows": (((zi + d) % NZ) * NX + xi) * NCORE + core} for d in range(1, NZ)]
    c_peers = [{"cols": (col + d) % NCOL} for d in range(1, NCOL)]
    peers = [core_peer] + x_peers + z_peers + c_peers

    barrier = pltpu.get_barrier_semaphore()
    for peer in peers:
        pl.semaphore_signal(barrier, inc=1, device_id=peer, device_id_type=MESH)

    load_wp = pltpu.make_async_copy(wp_hbm, wp, lsem.at[0])
    load_x = pltpu.make_async_copy(x_hbm, xb, lsem.at[1])
    load_g = pltpu.make_async_copy(g_hbm, gb, lsem.at[2])
    load_wo = pltpu.make_async_copy(wo_hbm, wo, lsem.at[3])
    load_wp.start()
    load_x.start()
    load_g.start()
    load_wo.start()

    def remote(src, dst, number, peer):
        return pltpu.make_async_remote_copy(
            src_ref=src, dst_ref=dst, send_sem=ssem.at[number], recv_sem=rsem.at[number],
            device_id=peer, device_id_type=MESH)

    zsel[...] = jnp.zeros_like(zsel)
    head_row = lax.broadcasted_iota(jnp.int32, (HEADS, E), 0)
    head_col = lax.broadcasted_iota(jnp.int32, (HEADS, E), 1) // (E // HEADS)
    zsel[ZERO_ROW:ZERO_ROW + HEADS, :] = (head_row == head_col).astype(F32).astype(BF16)

    def sel(off, cols):
        part = zsel[ZERO_ROW - off:ZERO_ROW - off + LANES, cols]
        return jnp.concatenate([part, part], axis=0)

    def chunk(n):
        return pl.ds(pl.multiple_of(n * NB, NB), NB)

    def spread(v, off):
        return mxu(split(v), sel(off, slice(0, E)))

    src_lane = lax.broadcasted_iota(jnp.int32, (LANES, 2 * LANES), 0)
    lane = lax.broadcasted_iota(jnp.int32, (LANES, 2 * LANES), 1)
    within = lane % 64
    h = within % 16
    want = 32 * (within // 16) + jnp.where(lane < 128, h, jnp.where(lane < 192, 16 + h // 2, 24 + h // 2))
    pick = (src_lane == want).astype(F32).astype(BF16)
    rate = rate_ref[...]
    rate_lane = jnp.concatenate([rate[k:k + 1, :] for k in range(4)] * 2, axis=1)
    load_wp.wait()
    w2 = mxu(wp[...], pick).astype(BF16)
    load_x.wait()
    proj = mxu(xb[...].reshape(PX, E), w2)
    pre = proj[:, :LANES]
    coef = proj[:, LANES:]
    step = jnp.maximum(pre, 0.0) + jnp.log1p(jnp.exp(-jnp.abs(pre)))
    logd = -rate_lane * step
    lane1 = lax.broadcasted_iota(jnp.int32, (PX, LANES), 1)
    c1 = jnp.where(lane1 < 64, step * coef, coef)
    c1f[...] = c1
    l_hl[...] = split(logd)
    d_hl[...] = split(jnp.exp(logd))
    c1_hl[...] = split(c1)

    logr = [logd[r * C:(r + 1) * C, :] for r in range(R)]
    up = [logr[0]]
    for r in range(1, R):
        up.append(up[-1] + logr[r])
    down = [logr[R - 1]]
    for r in range(R - 2, -1, -1):
        down.insert(0, down[0] + logr[r])
    zero = jnp.zeros((C, LANES), F32)
    lane2 = lax.broadcasted_iota(jnp.int32, (C, LANES), 1)
    falling = (lane2 % 64) >= 48
    for r in range(R):
        before = up[r - 1] if r else zero
        after = down[r + 1] if r < R - 1 else zero
        tail = jnp.where(falling, before, after)
        reach = jnp.where(falling, down[r], up[r])
        v = jnp.exp(jnp.where(lane2 < 64, tail, reach)) * c1[r * C:(r + 1) * C, :]
        v_hl[r] = split(v)
    fv[...] = jnp.exp(up[R - 1])

    def column_ends(start, i, dst):
        lhs = v_hl[:, pl.ds(start, HALF), :].reshape(R * HALF, 2 * LANES)
        for n in range(CHUNKS):
            cs = slice(n * NB, (n + 1) * NB)
            w = mxu(lhs, sel(32 + 16 * i, cs))
            acc = w[:HALF] * xb[0, pl.ds(start, HALF), cs].astype(F32)
            for r in range(1, R):
                acc = acc + w[r * HALF:(r + 1) * HALF] * xb[r, pl.ds(start, HALF), cs].astype(F32)
            dst[i, :, cs] = acc
        dst[i, :, E:] = fv[pl.ds(start, HALF), :]

    own = pl.multiple_of(core * HALF, HALF)
    other = pl.multiple_of((1 - core) * HALF, HALF)
    to_core = [remote(s0.at[i], ee.at[core, i], S_CORE + i, core_peer) for i in range(2)]
    for i in (1, 0):
        column_ends(other, i, s0)
        column_ends(own, i, ee.at[core])

    bt = lax.broadcasted_iota(jnp.int32, (256, 256), 0)
    bs = lax.broadcasted_iota(jnp.int32, (256, 256), 1)
    same = (bt // C) == (bs // C)
    behind = (same & (bs > bt)).astype(F32).astype(BF16)
    ahead = (same & (bs < bt)).astype(F32).astype(BF16)
    lane3 = lax.broadcasted_iota(jnp.int32, (256, LANES), 1)
    for m in range(PX // 256):
        ps = slice(m * 256, (m + 1) * 256)
        lh = l_hl[ps, :]
        a = mxu(behind, lh)
        b = mxu(ahead, lh)
        cum = jnp.where(lane3 < 16, a[:, :LANES] + a[:, LANES:], b[:, :LANES] + b[:, LANES:])
        h_hl[ps, :] = split(jnp.exp(cum) * c1f[ps, :])
    row_of = lax.broadcasted_iota(jnp.int32, (R, PX), 1) // C
    whole = (row_of == lax.broadcasted_iota(jnp.int32, (R, PX), 0)).astype(F32).astype(BF16)
    ft = mxu(whole, l_hl[...])
    ft = jnp.exp(ft[:, :LANES] + ft[:, LANES:])

    def row_ends(n, _):
        cs = chunk(n)
        for i in range(2):
            w = mxu(h_hl[...], sel(16 * i, cs)).reshape(R, C, NB)
            he[i, :, cs] = jnp.sum(w * xb[:, :, cs].astype(F32), axis=1)
        return 0

    lax.fori_loop(0, CHUNKS, row_ends, 0)
    for i in range(2):
        he[i, :, E:] = ft
    pl.semaphore_wait(barrier, len(peers))
    for i in (1, 0):
        to_core[i].start()

    load_g.wait()
    load_wo.wait()

    def gates(n, _):
        cs = chunk(n)
        gain = gain_ref[:, cs]
        for r in range(R):
            g = gb[r, :, cs].astype(F32)
            w = gain * (g / (1.0 + jnp.exp(-g)))
            for t in range(2):
                gg[2 * n + t, r * RS:r * RS + C, :] = w[:, t * LANES:(t + 1) * LANES]
        return 0

    lax.fori_loop(0, CHUNKS, gates, 0)

    to_x = [[remote(tt.at[x_dst[d], i], xe.at[xi, i], S_X + 3 * i + d, x_peers[d]) for d in range(NX - 1)]
            for i in range(2)]
    for i in (1, 0):
        to_core[i].wait_recv()
        first, second = ee.at[i, i], ee.at[1 - i, i]
        t = second[:, :E] + spread(second[:, E:], 32 + 16 * i) * first[:, :E]
        f = second[:, E:] * first[:, E:]
        for q in range(NX):
            tt[q, i, :, :E] = t[q * 8:(q + 1) * 8]
            tt[q, i, :, E:] = f[q * 8:(q + 1) * 8]
        for copy in to_x[i]:
            copy.start()
    xe[xi] = tt[xi]

    to_cols = [remote(he.at[(col + d) // NCOL], hr.at[col], S_COLS + d - 1, c_peers[d - 1])
               for d in range(1, NCOL)]
    for copy in to_cols:
        copy.start()
    hr[col] = he[0]

    def column_scans(n, _):
        cs = chunk(n)
        xs = [xb[r, :, cs].astype(F32) for r in range(R)]
        sk = skip_ref[:, cs]
        acc = [sk * xs[r] for r in range(R)]
        for i in range(2):
            off = 32 + 16 * i
            dd = mxu(d_hl[...], sel(off, cs))
            bb = mxu(c1_hl[...], sel(off, cs))
            oo = mxu(c1_hl[...], sel(64 + off, cs))
            state = None
            for r in (range(R) if i == 0 else range(R - 1, -1, -1)):
                ps = slice(r * C, (r + 1) * C)
                push = bb[ps] * xs[r]
                state = push if state is None else dd[ps] * state + push
                acc[r] = acc[r] + oo[ps] * state
        for r in range(R):
            for t in range(2):
                base[2 * n + t, r * RS:r * RS + C, :] = acc[r][:, t * LANES:(t + 1) * LANES]
        return 0

    lax.fori_loop(0, CHUNKS, column_scans, 0)

    def reach_spread(n, _):
        cs = chunk(n)
        vv = v_hl[...].reshape(PX, 2 * LANES)
        for off, dst in ((96, ro2), (112, ro3)):
            w = mxu(vv, sel(off, cs))
            for r in range(R):
                for t in range(2):
                    dst[2 * n + t, r * RS:r * RS + C, :] = w[r * C:(r + 1) * C, t * LANES:(t + 1) * LANES]
        return 0

    lax.fori_loop(0, CHUNKS, reach_spread, 0)

    to_z = [remote(tz.at[(zi + d) // NZ], ze.at[zi], S_Z + d - 1, z_peers[d - 1]) for d in range(1, NZ)]
    for i in (1, 0):
        for copy in to_x[i]:
            copy.wait_recv()
        fc = xe[0, i, :, E:]
        for q in range(1, NX):
            fc = fc * xe[q, i, :, E:]
        fs = spread(xe[:, i, :, E:].reshape(NX * 8, LANES), 32 + 16 * i)
        acc = jnp.zeros((8, E), F32)
        g = jnp.ones((8, E), F32)
        for q in (range(NX) if i == 0 else range(NX - 1, -1, -1)):
            f = fs[q * 8:(q + 1) * 8]
            px[i, q] = acc
            gx[i, q] = g
            acc = xe[q, i, :, :E] + f * acc
            g = g * f
        tz[i, :, :E] = acc
        tz[i, :, E:] = fc
        for d in range(1, NZ):
            @pl.when((zi + d) // NZ == i)
            def _():
                to_z[d - 1].start()
    ze[zi] = tz[0]

    for i in range(2):
        fxp[i] = spread(ee[i, i, :, E:], 32 + 16 * i)

    def back_copies(i, order):
        return [remote(sc.at[i, x_dst[d]], rc.at[i, xi], S_BACK + 3 * order + d, x_peers[d]) for d in range(NX - 1)]

    def over_groups(i, order):
        for d in range(1, NZ):
            @pl.when(1 - (zi + NZ - d) // NZ == i)
            def _():
                to_z[d - 1].wait_recv()
        before = zi + i * (NZ - 1 - 2 * zi)
        slots = []
        for m in range(NZ - 1):
            valid = (before + NZ - 1 - m) // NZ
            slots.append(valid * (m + i * (NZ - 1 - 2 * m)) + (1 - valid) * zi)
        at = pl.multiple_of(ZERO_ROW - 32 - 16 * i, 16)
        part = zsel[pl.ds(at, LANES), :]
        lhs = jnp.concatenate([ze[j, :, E:] for j in slots], axis=0)
        fs = mxu(split(lhs), jnp.concatenate([part, part], axis=0))
        acc = jnp.zeros((8, E), F32)
        for m, j in enumerate(slots):
            acc = jnp.where(m < before, ze[j, :, :E] + fs[m * 8:(m + 1) * 8] * acc, acc)
        for q in range(NX):
            sc[i, q] = px[i, q] + gx[i, q] * acc
        for copy in back_copies(i, order):
            copy.start()
        rc[i, xi] = sc[i, xi]

    def to_last(i, order):
        return remote(cc.at[1 - core, i], pc.at[i], S_LAST + order, core_peer)

    def over_chip(i, order):
        for copy in back_copies(i, order):
            copy.wait_recv()
        carry = rc[i].reshape(HALF, E)
        cc[i, i] = carry
        cc[1 - i, i] = ee[i, i, :, :E] + fxp[i] * carry
        to_last(i, order).start()

    near = zi // (NZ // 2)
    far = 1 - near

    def row_spread(n, _):
        cs = chunk(n)
        dv = d_hl[...]
        cv = c1_hl[...]
        xs = xb[:, :, cs].astype(F32)
        for lhs, off, drive, dst in ((dv, 0, 0, hd0), (cv, 0, 1, hb0), (cv, 64, 0, ho0),
                                     (dv, 16, 0, hd1), (cv, 16, 1, hb1), (cv, 80, 0, ho1)):
            w = mxu(lhs, sel(off, cs)).reshape(R, C, NB)
            if drive:
                w = w * xs
            for r in range(R):
                for t in range(2):
                    dst[2 * n + t, r * RS:r * RS + C, :] = w[r, :, t * LANES:(t + 1) * LANES]
        return 0

    lax.fori_loop(0, CHUNKS, row_spread, 0)
    for copy in to_cols:
        copy.wait_recv()
    fh = hr[:, :, E:].reshape(NCOL * R, LANES)
    f0 = spread(fh, 0)
    f1 = spread(fh, 16)
    in0 = jnp.zeros((R, E), F32)
    in1 = jnp.zeros((R, E), F32)
    for j in range(NCOL):
        in0 = jnp.where(j < col, hr[j, :, :E] + f0[j * R:(j + 1) * R] * in0, in0)
    for j in range(NCOL - 1, -1, -1):
        in1 = jnp.where(j > col, hr[j, :, :E] + f1[j * R:(j + 1) * R] * in1, in1)

    def row_step(c, states):
        out = []
        for at, hd, hb, ho, first in ((c, hd0, hb0, ho0, 0), (C - 1 - c, hd1, hb1, ho1, TILES)):
            ps = pl.ds(at, R, stride=RS)
            for t in range(TILES):
                s = hd[t, ps, :] * states[first + t] + hb[t, ps, :]
                base[t, ps, :] = base[t, ps, :] + ho[t, ps, :] * s
                out.append(s)
        return tuple(out)

    begin = [in0[:, t * LANES:(t + 1) * LANES] for t in range(TILES)]
    begin += [in1[:, t * LANES:(t + 1) * LANES] for t in range(TILES)]
    states = lax.fori_loop(0, C // 2, row_step, tuple(begin))
    over_groups(near, 0)
    over_groups(far, 1)
    lax.fori_loop(C // 2, C, row_step, states)
    over_chip(near, 0)
    over_chip(far, 1)

    def finish(start, carry):
        for part in range(2):
            for r in range(part * R // 2, (part + 1) * R // 2):
                ps = pl.ds(pl.multiple_of(r * RS + start, 8), HALF)
                tot = []
                sq = jnp.zeros((HALF, LANES), F32)
                for t in range(TILES):
                    ls = slice(t * LANES, (t + 1) * LANES)
                    v = base[t, ps, :] + ro2[t, ps, :] * carry[0, :, ls] + ro3[t, ps, :] * carry[1, :, ls]
                    sq = sq + v * v
                    tot.append(v)
                scale = lax.rsqrt(jnp.sum(sq, axis=-1, keepdims=True) * (1.0 / E) + 1e-05)
                for t in range(TILES):
                    ls = slice(t * LANES, (t + 1) * LANES)
                    nb[r, :, ls] = (tot[t] * scale * gg[t, ps, :]).astype(BF16)
            rs = slice(part * R // 2, (part + 1) * R // 2)
            res = mxu(nb[rs].reshape(R // 2 * HALF, E), wo[...])
            ob[rs, pl.ds(start, HALF), :] = res.astype(BF16).reshape(R // 2, HALF, D)

    finish(own, cc.at[core])
    for order, i in ((0, near), (1, far)):
        to_last(i, order).wait_recv()
    finish(other, pc)
    for copy in to_core + to_x[0] + to_x[1] + to_cols + to_z + back_copies(near, 0) + back_copies(far, 1):
        copy.wait_send()
    to_last(near, 0).wait_send()
    to_last(far, 1).wait_send()


def local(xin, gate_in, w_proj, rate, skip, norm_gain, w_out):
    vmem = pl.BlockSpec(memory_space=pltpu.VMEM)
    hbm = pl.BlockSpec(memory_space=pl.ANY)
    big = pltpu.VMEM((TILES, R * RS, LANES), F32)
    compact = pltpu.VMEM((PX, 2 * LANES), BF16)
    scratch = [
        pltpu.VMEM((R, C, E), BF16),
        pltpu.VMEM((R, C, E), BF16),
        pltpu.VMEM((E, LANES), BF16),
        pltpu.VMEM((E, D), BF16),
        pltpu.VMEM((ZERO_ROW + LANES, E), BF16),
        pltpu.VMEM((PX, LANES), F32),
        pltpu.VMEM((R, C, 2 * LANES), BF16),
        compact, compact, compact, compact,
        pltpu.VMEM((C, LANES), F32),
        big, big, big, big, big, big, big, big, big, big,
        pltpu.VMEM((2, HALF, WIDE), F32),
        pltpu.VMEM((2, 2, HALF, WIDE), F32),
        pltpu.VMEM((NX, 2, 8, WIDE), F32),
        pltpu.VMEM((NX, 2, 8, WIDE), F32),
        pltpu.VMEM((2, NX, 8, E), F32),
        pltpu.VMEM((2, NX, 8, E), F32),
        pltpu.VMEM((2, 8, WIDE), F32),
        pltpu.VMEM((NZ, 8, WIDE), F32),
        pltpu.VMEM((2, NX, 8, E), F32),
        pltpu.VMEM((2, NX, 8, E), F32),
        pltpu.VMEM((2, HALF, E), F32),
        pltpu.VMEM((2, 2, HALF, E), F32),
        pltpu.VMEM((2, HALF, E), F32),
        pltpu.VMEM((2, R, WIDE), F32),
        pltpu.VMEM((NCOL, R, WIDE), F32),
        pltpu.VMEM((R, HALF, E), BF16),
        pltpu.SemaphoreType.DMA((6,)),
        pltpu.SemaphoreType.DMA((N_SEM,)),
        pltpu.SemaphoreType.DMA((N_SEM,)),
    ]
    return pl.pallas_call(
        kernel,
        out_shape=pltpu.VMEM((R, C, D), BF16),
        in_specs=[hbm, hbm, hbm, vmem, vmem, vmem, hbm],
        out_specs=vmem,
        scratch_shapes=scratch,
        compiler_params=pltpu.CompilerParams(
            collective_id=0, has_side_effects=True, vmem_limit_bytes=60 * 1024 * 1024),
    )(xin, gate_in, w_proj, rate, skip.reshape(1, E), norm_gain.reshape(1, E), w_out)


def solution(mesh):
    in_specs = (P("rows", "cols", None), P("rows", "cols", None), P(), P(), P(), P(), P())
    return jax.shard_map(local, mesh=mesh, in_specs=in_specs, out_specs=P("rows", "cols", None), check_vma=False)
```

```python
import functools

import jax
import jax.numpy as jnp
from jax import lax
from jax.experimental import pallas as pl
from jax.experimental.pallas import tpu as pltpu
from jax.sharding import PartitionSpec as P

MESH = pl.DeviceIdType.MESH
F32 = jnp.float32
BF16 = jnp.bfloat16

R, C, E, D, HEADS = 8, 64, 1024, 512, 16
PX = R * C
HALF = C // 2
LANES = 128
TILES = E // LANES
WIDE = E + LANES
NB = 256
CHUNKS = E // NB
ZERO_ROW = 112
RS = 72

NZ, NX, NCORE, NCOL = 4, 4, 2, 8
FAR_FIRST = (1, 0, 2)

S_CORE, S_X, S_COLS, S_Z, S_BACK, S_LAST, N_SEM = 0, 2, 8, 15, 18, 24, 26


def split(v):
    hi = v.astype(BF16)
    lo = (v - hi.astype(F32)).astype(BF16)
    return jnp.concatenate([hi, lo], axis=-1)


def mxu(a, b):
    return jnp.dot(a, b, preferred_element_type=F32)


def kernel(x_hbm, g_hbm, wp_hbm, rate_hbm, skip_hbm, gain_hbm, wo_hbm, ob,
           xb, gb, wp, wo, rate_ref, skip_ref, gain_ref, zsel, c1f, v_hl, d_hl, c1_hl, l_hl, h_hl, fv,
           base, ro2, ro3, gg, hd0, hb0, ho0, hd1, hb1, ho1,
           s0, ee, tt, xe, px, gx, tz, ze, sc, rc, fxp, cc, pc, he, hr, nb,
           lsem, ssem, rsem):
    rows = lax.axis_index("rows")
    col = lax.axis_index("cols")
    core = rows % NCORE
    xi = (rows // NCORE) % NX
    zi = rows // (NCORE * NX)

    core_peer = {"rows": rows + 1 - 2 * core}
    x_dst = [(xi + d) % NX for d in range(1, NX)]
    x_peers = [{"rows": (zi * NX + t) * NCORE + core} for t in x_dst]
    z_peers = [{"rows": (((zi + d) % NZ) * NX + xi) * NCORE + core} for d in range(1, NZ)]
    c_peers = [{"cols": (col + d) % NCOL} for d in range(1, NCOL)]
    peers = [core_peer] + x_peers + z_peers + c_peers

    barrier = pltpu.get_barrier_semaphore()
    for peer in peers:
        pl.semaphore_signal(barrier, inc=1, device_id=peer, device_id_type=MESH)

    load_wp = pltpu.make_async_copy(wp_hbm, wp, lsem.at[0])
    load_x = pltpu.make_async_copy(x_hbm, xb, lsem.at[1])
    load_g = pltpu.make_async_copy(g_hbm, gb, lsem.at[2])
    load_wo = pltpu.make_async_copy(wo_hbm, wo, lsem.at[3])
    load_rate = pltpu.make_async_copy(rate_hbm, rate_ref, lsem.at[4])
    load_skip = pltpu.make_async_copy(skip_hbm, skip_ref, lsem.at[5])
    load_gain = pltpu.make_async_copy(gain_hbm, gain_ref, lsem.at[6])
    load_wp.start()
    load_x.start()
    load_rate.start()
    load_skip.start()
    load_gain.start()
    load_g.start()
    load_wo.start()

    def remote(src, dst, number, peer):
        return pltpu.make_async_remote_copy(
            src_ref=src, dst_ref=dst, send_sem=ssem.at[number], recv_sem=rsem.at[number],
            device_id=peer, device_id_type=MESH)

    zsel[...] = jnp.zeros_like(zsel)
    head_row = lax.broadcasted_iota(jnp.int32, (HEADS, E), 0)
    head_col = lax.broadcasted_iota(jnp.int32, (HEADS, E), 1) // (E // HEADS)
    zsel[ZERO_ROW:ZERO_ROW + HEADS, :] = (head_row == head_col).astype(F32).astype(BF16)

    def sel(off, cols):
        part = zsel[ZERO_ROW - off:ZERO_ROW - off + LANES, cols]
        return jnp.concatenate([part, part], axis=0)

    def chunk(n):
        return pl.ds(pl.multiple_of(n * NB, NB), NB)

    def spread(v, off):
        return mxu(split(v), sel(off, slice(0, E)))

    low = lax.broadcasted_iota(jnp.int32, (8, LANES), 1) < 64

    def spread_few(v, off):
        out = []
        for m in range(v.shape[0] // 8):
            row = v[m * 8:(m + 1) * 8]
            tiles = []
            for t in range(TILES):
                a = jnp.broadcast_to(row[:, off + 2 * t:off + 2 * t + 1], (8, LANES))
                b = jnp.broadcast_to(row[:, off + 2 * t + 1:off + 2 * t + 2], (8, LANES))
                tiles.append(jnp.where(low, a, b))
            out.append(jnp.concatenate(tiles, axis=1))
        return jnp.concatenate(out, axis=0)

    src_lane = lax.broadcasted_iota(jnp.int32, (LANES, 2 * LANES), 0)
    lane = lax.broadcasted_iota(jnp.int32, (LANES, 2 * LANES), 1)
    within = lane % 64
    h = within % 16
    want = 32 * (within // 16) + jnp.where(lane < 128, h, jnp.where(lane < 192, 16 + h // 2, 24 + h // 2))
    pick = (src_lane == want).astype(F32).astype(BF16)
    load_wp.wait()
    w2 = mxu(wp[...], pick).astype(BF16)
    load_rate.wait()
    rate = rate_ref[...]
    rate_lane = jnp.concatenate([rate[k:k + 1, :] for k in range(4)] * 2, axis=1)
    load_x.wait()
    proj = mxu(xb[...].reshape(PX, E), w2)
    pre = proj[:, :LANES]
    coef = proj[:, LANES:]
    step = jnp.maximum(pre, 0.0) + jnp.log1p(jnp.exp(-jnp.abs(pre)))
    logd = -rate_lane * step
    lane1 = lax.broadcasted_iota(jnp.int32, (PX, LANES), 1)
    c1 = jnp.where(lane1 < 64, step * coef, coef)
    c1f[...] = c1
    l_hl[...] = split(logd)
    d_hl[...] = split(jnp.exp(logd))
    c1_hl[...] = split(c1)

    logr = [logd[r * C:(r + 1) * C, :] for r in range(R)]
    up = [logr[0]]
    for r in range(1, R):
        up.append(up[-1] + logr[r])
    down = [logr[R - 1]]
    for r in range(R - 2, -1, -1):
        down.insert(0, down[0] + logr[r])
    zero = jnp.zeros((C, LANES), F32)
    lane2 = lax.broadcasted_iota(jnp.int32, (C, LANES), 1)
    falling = (lane2 % 64) >= 48
    for r in range(R):
        before = up[r - 1] if r else zero
        after = down[r + 1] if r < R - 1 else zero
        tail = jnp.where(falling, before, after)
        reach = jnp.where(falling, down[r], up[r])
        v = jnp.exp(jnp.where(lane2 < 64, tail, reach)) * c1[r * C:(r + 1) * C, :]
        v_hl[r] = split(v)
    fv[...] = jnp.exp(up[R - 1])

    def column_ends(start, i, dst):
        lhs = v_hl[:, pl.ds(start, HALF), :].reshape(R * HALF, 2 * LANES)
        for n in range(CHUNKS):
            cs = slice(n * NB, (n + 1) * NB)
            w = mxu(lhs, sel(32 + 16 * i, cs))
            acc = w[:HALF] * xb[0, pl.ds(start, HALF), cs].astype(F32)
            for r in range(1, R):
                acc = acc + w[r * HALF:(r + 1) * HALF] * xb[r, pl.ds(start, HALF), cs].astype(F32)
            dst[i, :, cs] = acc
        dst[i, :, E:] = fv[pl.ds(start, HALF), :]

    own = pl.multiple_of(core * HALF, HALF)
    other = pl.multiple_of((1 - core) * HALF, HALF)
    to_core = [remote(s0.at[i], ee.at[core, i], S_CORE + i, core_peer) for i in range(2)]
    column_ends(other, 1, s0)

    bt = lax.broadcasted_iota(jnp.int32, (256, 256), 0)
    bs = lax.broadcasted_iota(jnp.int32, (256, 256), 1)
    same = (bt // C) == (bs // C)
    behind = (same & (bs > bt)).astype(F32).astype(BF16)
    ahead = (same & (bs < bt)).astype(F32).astype(BF16)
    lane3 = lax.broadcasted_iota(jnp.int32, (256, LANES), 1)
    for m in range(PX // 256):
        ps = slice(m * 256, (m + 1) * 256)
        lh = l_hl[ps, :]
        a = mxu(behind, lh)
        b = mxu(ahead, lh)
        cum = jnp.where(lane3 < 16, a[:, :LANES] + a[:, LANES:], b[:, :LANES] + b[:, LANES:])
        h_hl[ps, :] = split(jnp.exp(cum) * c1f[ps, :])
    row_of = lax.broadcasted_iota(jnp.int32, (R, PX), 1) // C
    whole = (row_of == lax.broadcasted_iota(jnp.int32, (R, PX), 0)).astype(F32).astype(BF16)
    ft = mxu(whole, l_hl[...])
    ft = jnp.exp(ft[:, :LANES] + ft[:, LANES:])

    first = (NZ - zi) // NZ
    r_early = CHUNKS * ((NZ - 1 - zi) // (NZ // 2))
    c_early = CHUNKS // 2 * (first + (NZ - 1 - zi) // (NZ // 2))
    g_early = CHUNKS * first

    def row_ends(n, _):
        cs = chunk(n)
        for i in range(2):
            w = mxu(h_hl[...], sel(16 * i, cs)).reshape(R, C, NB)
            he[i, :, cs] = jnp.sum(w * xb[:, :, cs].astype(F32), axis=1)
        return 0

    lax.fori_loop(0, r_early, row_ends, 0)
    for i in range(2):
        he[i, :, E:] = ft

    load_skip.wait()
    load_gain.wait()

    def column_scans(n, _):
        cs = chunk(n)
        xs = [xb[r, :, cs].astype(F32) for r in range(R)]
        sk = skip_ref[:, cs]
        acc = [sk * xs[r] for r in range(R)]
        for i in range(2):
            off = 32 + 16 * i
            dd = mxu(d_hl[...], sel(off, cs))
            bb = mxu(c1_hl[...], sel(off, cs))
            oo = mxu(c1_hl[...], sel(64 + off, cs))
            state = None
            for r in (range(R) if i == 0 else range(R - 1, -1, -1)):
                ps = slice(r * C, (r + 1) * C)
                push = bb[ps] * xs[r]
                state = push if state is None else dd[ps] * state + push
                acc[r] = acc[r] + oo[ps] * state
        for r in range(R):
            for t in range(2):
                base[2 * n + t, r * RS:r * RS + C, :] = acc[r][:, t * LANES:(t + 1) * LANES]
        return 0

    lax.fori_loop(0, c_early, column_scans, 0)
    load_g.wait()
    load_wo.wait()

    def gates(n, _):
        cs = chunk(n)
        gain = gain_ref[:, cs]
        for r in range(R):
            g = gb[r, :, cs].astype(F32)
            w = gain * (g / (1.0 + jnp.exp(-g)))
            for t in range(2):
                gg[2 * n + t, r * RS:r * RS + C, :] = w[:, t * LANES:(t + 1) * LANES]
        return 0

    lax.fori_loop(0, g_early, gates, 0)

    pl.semaphore_wait(barrier, len(peers))
    to_core[1].start()
    column_ends(other, 0, s0)
    to_core[0].start()
    column_ends(own, 1, ee.at[core])
    column_ends(own, 0, ee.at[core])


    to_x = [[remote(tt.at[x_dst[d], i], xe.at[xi, i], S_X + 3 * i + d, x_peers[d]) for d in range(NX - 1)]
            for i in range(2)]

    def join_cores(i):
        to_core[i].wait_recv()
        first, second = ee.at[i, i], ee.at[1 - i, i]
        t = second[:, :E] + spread_few(second[:, E:], 32 + 16 * i) * first[:, :E]
        f = second[:, E:] * first[:, E:]
        for q in range(NX):
            tt[q, i, :, :E] = t[q * 8:(q + 1) * 8]
            tt[q, i, :, E:] = f[q * 8:(q + 1) * 8]
        for d in FAR_FIRST:
            to_x[i][d].start()
        xe[xi, i] = tt[xi, i]

    join_cores(1)
    lax.fori_loop(r_early, CHUNKS, row_ends, 0)
    to_cols = [remote(he.at[(col + d) // NCOL], hr.at[col], S_COLS + d - 1, c_peers[d - 1])
               for d in range(1, NCOL)]
    for copy in to_cols:
        copy.start()
    hr[col] = he[0]

    join_cores(0)
    lax.fori_loop(c_early, CHUNKS, column_scans, 0)


    def reach_spread(n, _):
        cs = chunk(n)
        vv = v_hl[...].reshape(PX, 2 * LANES)
        for off, dst in ((96, ro2), (112, ro3)):
            w = mxu(vv, sel(off, cs))
            for r in range(R):
                for t in range(2):
                    dst[2 * n + t, r * RS:r * RS + C, :] = w[r * C:(r + 1) * C, t * LANES:(t + 1) * LANES]
        return 0

    lax.fori_loop(g_early, r_early, gates, 0)
    lax.fori_loop(0, r_early, reach_spread, 0)

    def row_spread(n, _):
        cs = chunk(n)
        dv = d_hl[...]
        cv = c1_hl[...]
        xs = xb[:, :, cs].astype(F32)
        for lhs, off, drive, dst in ((dv, 0, 0, hd0), (cv, 0, 1, hb0), (cv, 64, 0, ho0),
                                     (dv, 16, 0, hd1), (cv, 16, 1, hb1), (cv, 80, 0, ho1)):
            w = mxu(lhs, sel(off, cs)).reshape(R, C, NB)
            if drive:
                w = w * xs
            for r in range(R):
                for t in range(2):
                    dst[2 * n + t, r * RS:r * RS + C, :] = w[r, :, t * LANES:(t + 1) * LANES]
        return 0

    lax.fori_loop(0, c_early, row_spread, 0)

    to_z = [remote(tz.at[(zi + d) // NZ], ze.at[zi], S_Z + d - 1, z_peers[d - 1]) for d in range(1, NZ)]
    for i in (1, 0):
        for copy in to_x[i]:
            copy.wait_recv()
        fc = xe[0, i, :, E:]
        for q in range(1, NX):
            fc = fc * xe[q, i, :, E:]
        fs = spread_few(xe[:, i, :, E:].reshape(NX * 8, LANES), 32 + 16 * i)
        acc = jnp.zeros((8, E), F32)
        g = jnp.ones((8, E), F32)
        for q in (range(NX) if i == 0 else range(NX - 1, -1, -1)):
            f = fs[q * 8:(q + 1) * 8]
            px[i, q] = acc
            gx[i, q] = g
            acc = xe[q, i, :, :E] + f * acc
            g = g * f
        tz[i, :, :E] = acc
        tz[i, :, E:] = pltpu.roll(fc, LANES - 32 - 16 * i, 1)
        for d in FAR_FIRST:
            @pl.when((zi + d + 1) // NZ == i)
            def _():
                to_z[d].start()
    ze[zi] = tz[0]

    for i in range(2):
        fxp[i] = spread(ee[i, i, :, E:], 32 + 16 * i)

    def back_copies(i, order):
        return [remote(sc.at[i, x_dst[d]], rc.at[i, xi], S_BACK + 3 * order + d, x_peers[d]) for d in range(NX - 1)]

    def over_groups(i, order):
        for d in range(1, NZ):
            @pl.when(1 - (zi + NZ - d) // NZ == i)
            def _():
                to_z[d - 1].wait_recv()
        before = zi + i * (NZ - 1 - 2 * zi)
        slots = []
        for m in range(NZ - 1):
            valid = (before + NZ - 1 - m) // NZ
            slots.append(valid * (m + i * (NZ - 1 - 2 * m)) + (1 - valid) * zi)
        fs = spread_few(jnp.concatenate([ze[j, :, E:] for j in slots], axis=0), 0)
        acc = jnp.zeros((8, E), F32)
        for m, j in enumerate(slots):
            acc = jnp.where(m < before, ze[j, :, :E] + fs[m * 8:(m + 1) * 8] * acc, acc)
        for q in range(NX):
            sc[i, q] = px[i, q] + gx[i, q] * acc
        copies = back_copies(i, order)
        for d in FAR_FIRST:
            copies[d].start()
        rc[i, xi] = sc[i, xi]

    def to_last(i, order):
        return remote(cc.at[1 - core, i], pc.at[i], S_LAST + order, core_peer)

    def over_chip(i, order):
        for copy in back_copies(i, order):
            copy.wait_recv()
        carry = rc[i].reshape(HALF, E)
        cc[i, i] = carry
        cc[1 - i, i] = ee[i, i, :, :E] + fxp[i] * carry
        to_last(i, order).start()

    near = zi // (NZ // 2)
    far = 1 - near

    edge = zi % (NZ - 1) == 0

    @pl.when(edge)
    def _():
        over_groups(near, 0)

    lax.fori_loop(c_early, CHUNKS, row_spread, 0)
    for copy in to_cols:
        copy.wait_recv()
    fh = hr[:, :, E:].reshape(NCOL * R, LANES)
    f0 = spread(fh, 0)
    f1 = spread(fh, 16)
    in0 = jnp.zeros((R, E), F32)
    in1 = jnp.zeros((R, E), F32)
    for j in range(NCOL):
        in0 = jnp.where(j < col, hr[j, :, :E] + f0[j * R:(j + 1) * R] * in0, in0)
    for j in range(NCOL - 1, -1, -1):
        in1 = jnp.where(j > col, hr[j, :, :E] + f1[j * R:(j + 1) * R] * in1, in1)

    def row_step(c, states):
        out = []
        for at, hd, hb, ho, first in ((c, hd0, hb0, ho0, 0), (C - 1 - c, hd1, hb1, ho1, TILES)):
            ps = pl.ds(at, R, stride=RS)
            for t in range(TILES):
                s = hd[t, ps, :] * states[first + t] + hb[t, ps, :]
                base[t, ps, :] = base[t, ps, :] + ho[t, ps, :] * s
                out.append(s)
        return tuple(out)

    begin = [in0[:, t * LANES:(t + 1) * LANES] for t in range(TILES)]
    begin += [in1[:, t * LANES:(t + 1) * LANES] for t in range(TILES)]
    states = lax.fori_loop(0, C // 2, row_step, tuple(begin))

    @pl.when(edge)
    def _():
        over_chip(near, 0)

    @pl.when(jnp.logical_not(edge))
    def _():
        over_groups(near, 0)

    over_groups(far, 1)
    lax.fori_loop(C // 2, C, row_step, states)
    lax.fori_loop(r_early, CHUNKS, gates, 0)
    lax.fori_loop(r_early, CHUNKS, reach_spread, 0)

    @pl.when(jnp.logical_not(edge))
    def _():
        over_chip(near, 0)

    over_chip(far, 1)

    def finish(start, carry):
        for part in range(2):
            for r in range(part * R // 2, (part + 1) * R // 2):
                ps = pl.ds(pl.multiple_of(r * RS + start, 8), HALF)
                tot = []
                sq = jnp.zeros((HALF, LANES), F32)
                for t in range(TILES):
                    ls = slice(t * LANES, (t + 1) * LANES)
                    v = base[t, ps, :] + ro2[t, ps, :] * carry[0, :, ls] + ro3[t, ps, :] * carry[1, :, ls]
                    sq = sq + v * v
                    tot.append(v)
                scale = lax.rsqrt(jnp.sum(sq, axis=-1, keepdims=True) * (1.0 / E) + 1e-05)
                for t in range(TILES):
                    ls = slice(t * LANES, (t + 1) * LANES)
                    nb[r, :, ls] = (tot[t] * scale * gg[t, ps, :]).astype(BF16)
            rs = slice(part * R // 2, (part + 1) * R // 2)
            res = mxu(nb[rs].reshape(R // 2 * HALF, E), wo[...])
            ob[rs, pl.ds(start, HALF), :] = res.astype(BF16).reshape(R // 2, HALF, D)

    finish(own, cc.at[core])
    for order, i in ((0, near), (1, far)):
        to_last(i, order).wait_recv()
    finish(other, pc)
    for copy in to_core + to_x[0] + to_x[1] + to_cols + to_z + back_copies(near, 0) + back_copies(far, 1):
        copy.wait_send()
    to_last(near, 0).wait_send()
    to_last(far, 1).wait_send()


def local(xin, gate_in, w_proj, rate, skip, norm_gain, w_out):
    vmem = pl.BlockSpec(memory_space=pltpu.VMEM)
    hbm = pl.BlockSpec(memory_space=pl.ANY)
    big = pltpu.VMEM((TILES, R * RS, LANES), F32)
    compact = pltpu.VMEM((PX, 2 * LANES), BF16)
    scratch = [
        pltpu.VMEM((R, C, E), BF16),
        pltpu.VMEM((R, C, E), BF16),
        pltpu.VMEM((E, LANES), BF16),
        pltpu.VMEM((E, D), BF16),
        pltpu.VMEM((4, HEADS), F32),
        pltpu.VMEM((1, E), F32),
        pltpu.VMEM((1, E), F32),
        pltpu.VMEM((ZERO_ROW + LANES, E), BF16),
        pltpu.VMEM((PX, LANES), F32),
        pltpu.VMEM((R, C, 2 * LANES), BF16),
        compact, compact, compact, compact,
        pltpu.VMEM((C, LANES), F32),
        big, big, big, big, big, big, big, big, big, big,
        pltpu.VMEM((2, HALF, WIDE), F32),
        pltpu.VMEM((2, 2, HALF, WIDE), F32),
        pltpu.VMEM((NX, 2, 8, WIDE), F32),
        pltpu.VMEM((NX, 2, 8, WIDE), F32),
        pltpu.VMEM((2, NX, 8, E), F32),
        pltpu.VMEM((2, NX, 8, E), F32),
        pltpu.VMEM((2, 8, WIDE), F32),
        pltpu.VMEM((NZ, 8, WIDE), F32),
        pltpu.VMEM((2, NX, 8, E), F32),
        pltpu.VMEM((2, NX, 8, E), F32),
        pltpu.VMEM((2, HALF, E), F32),
        pltpu.VMEM((2, 2, HALF, E), F32),
        pltpu.VMEM((2, HALF, E), F32),
        pltpu.VMEM((2, R, WIDE), F32),
        pltpu.VMEM((NCOL, R, WIDE), F32),
        pltpu.VMEM((R, HALF, E), BF16),
        pltpu.SemaphoreType.DMA((7,)),
        pltpu.SemaphoreType.DMA((N_SEM,)),
        pltpu.SemaphoreType.DMA((N_SEM,)),
    ]
    return pl.pallas_call(
        kernel,
        out_shape=pltpu.VMEM((R, C, D), BF16),
        in_specs=[hbm] * 7,
        out_specs=vmem,
        scratch_shapes=scratch,
        compiler_params=pltpu.CompilerParams(
            collective_id=0, has_side_effects=True, vmem_limit_bytes=60 * 1024 * 1024),
    )(xin, gate_in, w_proj, rate, skip.reshape(1, E), norm_gain.reshape(1, E), w_out)


def solution(mesh):
    in_specs = (P("rows", "cols", None), P("rows", "cols", None), P(), P(), P(), P(), P())
    return jax.shard_map(local, mesh=mesh, in_specs=in_specs, out_specs=P("rows", "cols", None), check_vma=False)
```

```python
import functools

import jax
import jax.numpy as jnp
from jax import lax
from jax.experimental import pallas as pl
from jax.experimental.pallas import tpu as pltpu
from jax.sharding import PartitionSpec as P

MESH = pl.DeviceIdType.MESH
F32 = jnp.float32
BF16 = jnp.bfloat16

R, C, E, D, HEADS = 8, 64, 1024, 512, 16
PX = R * C
HALF = C // 2
LANES = 128
PART = 16
TILES = E // LANES
WIDE = E + LANES
NB = 256
CHUNKS = E // NB
ZERO_ROW = 112
RS = 72

NZ, NX, NCORE, NCOL = 4, 4, 2, 8
FAR_FIRST = (1, 0, 2)

S_CORE, S_X, S_COLS, S_Z, S_BACK, S_LAST, N_SEM = 0, 2, 8, 15, 18, 24, 27


def split(v):
    hi = v.astype(BF16)
    lo = (v - hi.astype(F32)).astype(BF16)
    return jnp.concatenate([hi, lo], axis=-1)


def mxu(a, b):
    return jnp.dot(a, b, preferred_element_type=F32)


def kernel(x_hbm, g_hbm, wp_hbm, rate_hbm, skip_hbm, gain_hbm, wo_hbm, ob,
           xb, gb, wp, wo, rate_ref, skip_ref, gain_ref, zsel, c1f, v_hl, d_hl, c1_hl, l_hl, h_hl, fv,
           base, ro2, ro3, gg, hd0, hb0, ho0, hd1, hb1, ho1,
           s0, ee, tt, xe, px, gx, tz, ze, sc, rc, fxp, cc, pc, he, hr, nb,
           lsem, ssem, rsem, gsem):
    rows = lax.axis_index("rows")
    col = lax.axis_index("cols")
    core = rows % NCORE
    xi = (rows // NCORE) % NX
    zi = rows // (NCORE * NX)

    core_peer = {"rows": rows + 1 - 2 * core}
    x_dst = [(xi + d) % NX for d in range(1, NX)]
    x_peers = [{"rows": (zi * NX + t) * NCORE + core} for t in x_dst]
    z_peers = [{"rows": (((zi + d) % NZ) * NX + xi) * NCORE + core} for d in range(1, NZ)]
    c_peers = [{"cols": (col + d) % NCOL} for d in range(1, NCOL)]
    def greeter(peer):
        peer_rows = peer.get("rows", rows)
        return {"rows": peer_rows - peer_rows % NCORE + 1, "cols": peer.get("cols", col)}

    outside = [greeter(peer) for peer in x_peers + z_peers + c_peers]
    barrier = pltpu.get_barrier_semaphore()

    @pl.when(core == 1)
    def _():
        pl.semaphore_signal(barrier, inc=1, device_id=core_peer, device_id_type=MESH)

    for peer in outside:
        pl.semaphore_signal(barrier, inc=1, device_id=peer, device_id_type=MESH)

    def wait_for_core():
        @pl.when(core == 0)
        def _():
            pl.semaphore_wait(barrier, 1)
            pl.semaphore_signal(gsem.at[0], inc=1, device_id=core_peer, device_id_type=MESH)

        @pl.when(core == 1)
        def _():
            pl.semaphore_wait(gsem.at[0], 1)

    def wait_for_others():
        @pl.when(core == 1)
        def _():
            pl.semaphore_wait(barrier, NCORE * len(outside))
            pl.semaphore_signal(gsem.at[1], inc=1, device_id=core_peer, device_id_type=MESH)

        @pl.when(core == 0)
        def _():
            pl.semaphore_wait(gsem.at[1], 1)

    load_wp = pltpu.make_async_copy(wp_hbm, wp, lsem.at[0])
    load_x = pltpu.make_async_copy(x_hbm, xb, lsem.at[1])
    load_g = pltpu.make_async_copy(g_hbm, gb, lsem.at[2])
    load_wo = pltpu.make_async_copy(wo_hbm, wo, lsem.at[3])
    load_rate = pltpu.make_async_copy(rate_hbm, rate_ref, lsem.at[4])
    load_skip = pltpu.make_async_copy(skip_hbm, skip_ref, lsem.at[5])
    load_gain = pltpu.make_async_copy(gain_hbm, gain_ref, lsem.at[6])
    load_wp.start()
    load_x.start()
    load_rate.start()
    load_skip.start()
    load_gain.start()
    load_g.start()
    load_wo.start()

    def remote(src, dst, number, peer):
        return pltpu.make_async_remote_copy(
            src_ref=src, dst_ref=dst, send_sem=ssem.at[number], recv_sem=rsem.at[number],
            device_id=peer, device_id_type=MESH)

    zsel[...] = jnp.zeros_like(zsel)
    head_row = lax.broadcasted_iota(jnp.int32, (HEADS, E), 0)
    head_col = lax.broadcasted_iota(jnp.int32, (HEADS, E), 1) // (E // HEADS)
    zsel[ZERO_ROW:ZERO_ROW + HEADS, :] = (head_row == head_col).astype(F32).astype(BF16)

    def sel(off, cols):
        part = zsel[ZERO_ROW - off:ZERO_ROW - off + LANES, cols]
        return jnp.concatenate([part, part], axis=0)

    def chunk(n):
        return pl.ds(pl.multiple_of(n * NB, NB), NB)

    def spread(v, off):
        return mxu(split(v), sel(off, slice(0, E)))

    low = lax.broadcasted_iota(jnp.int32, (8, LANES), 1) < 64

    def spread_few(v, off):
        out = []
        for m in range(v.shape[0] // 8):
            row = v[m * 8:(m + 1) * 8]
            tiles = []
            for t in range(TILES):
                a = jnp.broadcast_to(row[:, off + 2 * t:off + 2 * t + 1], (8, LANES))
                b = jnp.broadcast_to(row[:, off + 2 * t + 1:off + 2 * t + 2], (8, LANES))
                tiles.append(jnp.where(low, a, b))
            out.append(jnp.concatenate(tiles, axis=1))
        return jnp.concatenate(out, axis=0)

    src_lane = lax.broadcasted_iota(jnp.int32, (LANES, 2 * LANES), 0)
    lane = lax.broadcasted_iota(jnp.int32, (LANES, 2 * LANES), 1)
    within = lane % 64
    h = within % 16
    want = 32 * (within // 16) + jnp.where(lane < 128, h, jnp.where(lane < 192, 16 + h // 2, 24 + h // 2))
    pick = (src_lane == want).astype(F32).astype(BF16)
    load_wp.wait()
    w2 = mxu(wp[...], pick).astype(BF16)
    load_rate.wait()
    rate = rate_ref[...]
    rate_lane = jnp.concatenate([rate[k:k + 1, :] for k in range(4)] * 2, axis=1)
    load_x.wait()
    proj = mxu(xb[...].reshape(PX, E), w2)
    pre = proj[:, :LANES]
    coef = proj[:, LANES:]
    step = jnp.maximum(pre, 0.0) + jnp.log1p(jnp.exp(-jnp.abs(pre)))
    logd = -rate_lane * step
    lane1 = lax.broadcasted_iota(jnp.int32, (PX, LANES), 1)
    c1 = jnp.where(lane1 < 64, step * coef, coef)
    c1f[...] = c1
    l_hl[...] = split(logd)
    d_hl[...] = split(jnp.exp(logd))
    c1_hl[...] = split(c1)

    logr = [logd[r * C:(r + 1) * C, :] for r in range(R)]
    up = [logr[0]]
    for r in range(1, R):
        up.append(up[-1] + logr[r])
    down = [logr[R - 1]]
    for r in range(R - 2, -1, -1):
        down.insert(0, down[0] + logr[r])
    zero = jnp.zeros((C, LANES), F32)
    lane2 = lax.broadcasted_iota(jnp.int32, (C, LANES), 1)
    falling = (lane2 % 64) >= 48
    for r in range(R):
        before = up[r - 1] if r else zero
        after = down[r + 1] if r < R - 1 else zero
        tail = jnp.where(falling, before, after)
        reach = jnp.where(falling, down[r], up[r])
        v = jnp.exp(jnp.where(lane2 < 64, tail, reach)) * c1[r * C:(r + 1) * C, :]
        v_hl[r] = split(v)
    fv[...] = jnp.exp(up[R - 1])

    def column_ends(start, i, dst):
        lhs = v_hl[:, pl.ds(start, HALF), :].reshape(R * HALF, 2 * LANES)
        for n in range(CHUNKS):
            cs = slice(n * NB, (n + 1) * NB)
            w = mxu(lhs, sel(32 + 16 * i, cs))
            acc = w[:HALF] * xb[0, pl.ds(start, HALF), cs].astype(F32)
            for r in range(1, R):
                acc = acc + w[r * HALF:(r + 1) * HALF] * xb[r, pl.ds(start, HALF), cs].astype(F32)
            dst[i, :, cs] = acc
        dst[i, :, E:] = fv[pl.ds(start, HALF), :]

    own = pl.multiple_of(core * HALF, HALF)
    other = pl.multiple_of((1 - core) * HALF, HALF)
    to_core = [remote(s0.at[i], ee.at[core, i], S_CORE + i, core_peer) for i in range(2)]
    column_ends(other, 1, s0)

    bt = lax.broadcasted_iota(jnp.int32, (256, 256), 0)
    bs = lax.broadcasted_iota(jnp.int32, (256, 256), 1)
    same = (bt // C) == (bs // C)
    behind = (same & (bs > bt)).astype(F32).astype(BF16)
    ahead = (same & (bs < bt)).astype(F32).astype(BF16)
    lane3 = lax.broadcasted_iota(jnp.int32, (256, LANES), 1)
    for m in range(PX // 256):
        ps = slice(m * 256, (m + 1) * 256)
        lh = l_hl[ps, :]
        a = mxu(behind, lh)
        b = mxu(ahead, lh)
        cum = jnp.where(lane3 < 16, a[:, :LANES] + a[:, LANES:], b[:, :LANES] + b[:, LANES:])
        h_hl[ps, :] = split(jnp.exp(cum) * c1f[ps, :])
    row_of = lax.broadcasted_iota(jnp.int32, (R, PX), 1) // C
    whole = (row_of == lax.broadcasted_iota(jnp.int32, (R, PX), 0)).astype(F32).astype(BF16)
    ft = mxu(whole, l_hl[...])
    ft = jnp.exp(ft[:, :LANES] + ft[:, LANES:])

    first = (NZ - zi) // NZ
    r_early = CHUNKS * ((NZ - 1 - zi) // (NZ // 2))
    c_early = CHUNKS // 2 * (first + (NZ - 1 - zi) // (NZ // 2))
    g_early = CHUNKS * first

    def row_ends(n, _):
        cs = chunk(n)
        for i in range(2):
            w = mxu(h_hl[...], sel(16 * i, cs)).reshape(R, C, NB)
            he[i, :, cs] = jnp.sum(w * xb[:, :, cs].astype(F32), axis=1)
        return 0

    lax.fori_loop(0, r_early, row_ends, 0)
    for i in range(2):
        he[i, :, E:] = ft

    load_skip.wait()
    load_gain.wait()

    def column_scans(n, _):
        cs = chunk(n)
        xs = [xb[r, :, cs].astype(F32) for r in range(R)]
        sk = skip_ref[:, cs]
        acc = [sk * xs[r] for r in range(R)]
        for i in range(2):
            off = 32 + 16 * i
            dd = mxu(d_hl[...], sel(off, cs))
            bb = mxu(c1_hl[...], sel(off, cs))
            oo = mxu(c1_hl[...], sel(64 + off, cs))
            state = None
            for r in (range(R) if i == 0 else range(R - 1, -1, -1)):
                ps = slice(r * C, (r + 1) * C)
                push = bb[ps] * xs[r]
                state = push if state is None else dd[ps] * state + push
                acc[r] = acc[r] + oo[ps] * state
        for r in range(R):
            for t in range(2):
                base[2 * n + t, r * RS:r * RS + C, :] = acc[r][:, t * LANES:(t + 1) * LANES]
        return 0

    lax.fori_loop(0, c_early, column_scans, 0)
    load_g.wait()
    load_wo.wait()

    def gates(n, _):
        cs = chunk(n)
        gain = gain_ref[:, cs]
        for r in range(R):
            g = gb[r, :, cs].astype(F32)
            w = gain * (g / (1.0 + jnp.exp(-g)))
            for t in range(2):
                gg[2 * n + t, r * RS:r * RS + C, :] = w[:, t * LANES:(t + 1) * LANES]
        return 0

    lax.fori_loop(0, g_early, gates, 0)

    wait_for_core()
    to_core[1].start()
    column_ends(other, 0, s0)
    to_core[0].start()
    column_ends(own, 1, ee.at[core])
    column_ends(own, 0, ee.at[core])


    to_x = [[remote(tt.at[x_dst[d], i], xe.at[xi, i], S_X + 3 * i + d, x_peers[d]) for d in range(NX - 1)]
            for i in range(2)]

    def join_cores(i):
        to_core[i].wait_recv()
        first, second = ee.at[i, i], ee.at[1 - i, i]
        t = second[:, :E] + spread_few(second[:, E:], 32 + 16 * i) * first[:, :E]
        f = second[:, E:] * first[:, E:]
        for q in range(NX):
            tt[q, i, :, :E] = t[q * 8:(q + 1) * 8]
            tt[q, i, :, E:] = f[q * 8:(q + 1) * 8]
        if i == 1:
            wait_for_others()
        for d in FAR_FIRST:
            to_x[i][d].start()
        xe[xi, i] = tt[xi, i]

    join_cores(1)
    lax.fori_loop(r_early, CHUNKS, row_ends, 0)
    to_cols = [remote(he.at[(col + d) // NCOL], hr.at[col], S_COLS + d - 1, c_peers[d - 1])
               for d in range(1, NCOL)]
    for copy in to_cols:
        copy.start()
    hr[col] = he[0]

    join_cores(0)
    lax.fori_loop(c_early, CHUNKS, column_scans, 0)


    def reach_spread(n, _):
        cs = chunk(n)
        vv = v_hl[...].reshape(PX, 2 * LANES)
        for off, dst in ((96, ro2), (112, ro3)):
            w = mxu(vv, sel(off, cs))
            for r in range(R):
                for t in range(2):
                    dst[2 * n + t, r * RS:r * RS + C, :] = w[r * C:(r + 1) * C, t * LANES:(t + 1) * LANES]
        return 0

    lax.fori_loop(g_early, r_early, gates, 0)
    lax.fori_loop(0, r_early, reach_spread, 0)

    def row_spread(n, _):
        cs = chunk(n)
        dv = d_hl[...]
        cv = c1_hl[...]
        xs = xb[:, :, cs].astype(F32)
        for lhs, off, drive, dst in ((dv, 0, 0, hd0), (cv, 0, 1, hb0), (cv, 64, 0, ho0),
                                     (dv, 16, 0, hd1), (cv, 16, 1, hb1), (cv, 80, 0, ho1)):
            w = mxu(lhs, sel(off, cs)).reshape(R, C, NB)
            if drive:
                w = w * xs
            for r in range(R):
                for t in range(2):
                    dst[2 * n + t, r * RS:r * RS + C, :] = w[r, :, t * LANES:(t + 1) * LANES]
        return 0

    lax.fori_loop(0, c_early, row_spread, 0)

    to_z = [remote(tz.at[(zi + d) // NZ], ze.at[zi], S_Z + d - 1, z_peers[d - 1]) for d in range(1, NZ)]
    for i in (1, 0):
        for copy in to_x[i]:
            copy.wait_recv()
        fc = xe[0, i, :, E:]
        for q in range(1, NX):
            fc = fc * xe[q, i, :, E:]
        fs = spread_few(xe[:, i, :, E:].reshape(NX * 8, LANES), 32 + 16 * i)
        acc = jnp.zeros((8, E), F32)
        g = jnp.ones((8, E), F32)
        for q in (range(NX) if i == 0 else range(NX - 1, -1, -1)):
            f = fs[q * 8:(q + 1) * 8]
            px[i, q] = acc
            gx[i, q] = g
            acc = xe[q, i, :, :E] + f * acc
            g = g * f
        tz[i, :, :E] = acc
        tz[i, :, E:] = pltpu.roll(fc, LANES - 32 - 16 * i, 1)
        for d in FAR_FIRST:
            @pl.when((zi + d + 1) // NZ == i)
            def _():
                to_z[d].start()
    ze[zi] = tz[0]

    for i in range(2):
        fxp[i] = spread(ee[i, i, :, E:], 32 + 16 * i)

    def back_copies(i, order):
        return [remote(sc.at[i, x_dst[d]], rc.at[i, xi], S_BACK + 3 * order + d, x_peers[d]) for d in range(NX - 1)]

    def over_groups(i, order):
        for d in range(1, NZ):
            @pl.when(1 - (zi + NZ - d) // NZ == i)
            def _():
                to_z[d - 1].wait_recv()
        before = zi + i * (NZ - 1 - 2 * zi)
        slots = []
        for m in range(NZ - 1):
            valid = (before + NZ - 1 - m) // NZ
            slots.append(valid * (m + i * (NZ - 1 - 2 * m)) + (1 - valid) * zi)
        fs = spread_few(jnp.concatenate([ze[j, :, E:] for j in slots], axis=0), 0)
        acc = jnp.zeros((8, E), F32)
        for m, j in enumerate(slots):
            acc = jnp.where(m < before, ze[j, :, :E] + fs[m * 8:(m + 1) * 8] * acc, acc)
        for q in range(NX):
            sc[i, q] = px[i, q] + gx[i, q] * acc
        copies = back_copies(i, order)
        for d in FAR_FIRST:
            copies[d].start()
        rc[i, xi] = sc[i, xi]

    def to_last(i, order):
        return remote(cc.at[1 - core, i], pc.at[i], S_LAST + order, core_peer)

    def over_chip(i, order):
        for copy in back_copies(i, order):
            copy.wait_recv()
        carry = rc[i].reshape(HALF, E)
        cc[i, i] = carry
        cc[1 - i, i] = ee[i, i, :, :E] + fxp[i] * carry
        to_last(i, order).start()

    near = zi // (NZ // 2)
    far = 1 - near

    edge = zi % (NZ - 1) == 0

    @pl.when(edge)
    def _():
        over_groups(near, 0)

    lax.fori_loop(c_early, CHUNKS, row_spread, 0)
    for copy in to_cols:
        copy.wait_recv()
    fh = hr[:, :, E:].reshape(NCOL * R, LANES)
    f0 = spread(fh, 0)
    f1 = spread(fh, 16)
    in0 = jnp.zeros((R, E), F32)
    in1 = jnp.zeros((R, E), F32)
    for j in range(NCOL):
        in0 = jnp.where(j < col, hr[j, :, :E] + f0[j * R:(j + 1) * R] * in0, in0)
    for j in range(NCOL - 1, -1, -1):
        in1 = jnp.where(j > col, hr[j, :, :E] + f1[j * R:(j + 1) * R] * in1, in1)

    def row_step(c, states):
        out = []
        for at, hd, hb, ho, first in ((c, hd0, hb0, ho0, 0), (C - 1 - c, hd1, hb1, ho1, TILES)):
            ps = pl.ds(at, R, stride=RS)
            for t in range(TILES):
                s = hd[t, ps, :] * states[first + t] + hb[t, ps, :]
                base[t, ps, :] = base[t, ps, :] + ho[t, ps, :] * s
                out.append(s)
        return tuple(out)

    begin = [in0[:, t * LANES:(t + 1) * LANES] for t in range(TILES)]
    begin += [in1[:, t * LANES:(t + 1) * LANES] for t in range(TILES)]
    states = lax.fori_loop(0, C // 2, row_step, tuple(begin))

    @pl.when(jnp.logical_not(edge))
    def _():
        over_groups(near, 0)

    over_groups(far, 1)
    lax.fori_loop(C // 2, C, row_step, states)
    lax.fori_loop(r_early, CHUNKS, gates, 0)
    lax.fori_loop(r_early, CHUNKS, reach_spread, 0)
    over_chip(near, 0)

    odd = xi % 2

    def arrived(d):
        remote(sc.at[far, xi], rc.at[far, xi], S_BACK + 3 + d, x_peers[1]).wait_recv()

    def last_part(p):
        cs = pl.ds(starts[p], PART)
        return remote(cc.at[1 - core, far, cs], pc.at[far, cs], S_LAST + 1 + p, core_peer)

    def over_chip_part(p):
        cs = pl.ds(starts[p], PART)
        carry = rc[far, pl.ds(starts[p] // 8, PART // 8)].reshape(PART, E)
        cc[far, far, cs, :] = carry
        cc[1 - far, far, cs, :] = ee[far, far, cs, :E] + fxp[far, cs, :] * carry
        last_part(p).start()

    group = xi // 2
    starts = [pl.multiple_of(group * PART, PART), pl.multiple_of((1 - group) * PART, PART)]

    def finish(start, carry, p):
        cs = pl.ds(starts[p], PART)
        for r in range(R):
            ps = pl.ds(pl.multiple_of(r * RS + start + starts[p], 8), PART)
            tot = []
            sq = jnp.zeros((PART, LANES), F32)
            for t in range(TILES):
                ls = slice(t * LANES, (t + 1) * LANES)
                v = base[t, ps, :] + ro2[t, ps, :] * carry[0, cs, ls] + ro3[t, ps, :] * carry[1, cs, ls]
                sq = sq + v * v
                tot.append(v)
            scale = lax.rsqrt(jnp.sum(sq, axis=-1, keepdims=True) * (1.0 / E) + 1e-05)
            for t in range(TILES):
                ls = slice(t * LANES, (t + 1) * LANES)
                nb[r, :, ls] = (tot[t] * scale * gg[t, ps, :]).astype(BF16)
        res = mxu(nb[...].reshape(R * PART, E), wo[...])
        at = pl.multiple_of(start + starts[p], PART)
        ob[:, pl.ds(at, PART), :] = res.astype(BF16).reshape(R, PART, D)

    arrived(2 - 2 * odd)
    over_chip_part(0)
    finish(own, cc.at[core], 0)
    arrived(1)
    arrived(2 * odd)
    over_chip_part(1)
    finish(own, cc.at[core], 1)
    to_last(near, 0).wait_recv()
    for p in range(2):
        last_part(p).wait_recv()
        finish(other, pc, p)
    for copy in to_core + to_x[0] + to_x[1] + to_cols + to_z + back_copies(near, 0) + back_copies(far, 1):
        copy.wait_send()
    to_last(near, 0).wait_send()
    for p in range(2):
        last_part(p).wait_send()


def local(xin, gate_in, w_proj, rate, skip, norm_gain, w_out):
    vmem = pl.BlockSpec(memory_space=pltpu.VMEM)
    hbm = pl.BlockSpec(memory_space=pl.ANY)
    big = pltpu.VMEM((TILES, R * RS, LANES), F32)
    compact = pltpu.VMEM((PX, 2 * LANES), BF16)
    scratch = [
        pltpu.VMEM((R, C, E), BF16),
        pltpu.VMEM((R, C, E), BF16),
        pltpu.VMEM((E, LANES), BF16),
        pltpu.VMEM((E, D), BF16),
        pltpu.VMEM((4, HEADS), F32),
        pltpu.VMEM((1, E), F32),
        pltpu.VMEM((1, E), F32),
        pltpu.VMEM((ZERO_ROW + LANES, E), BF16),
        pltpu.VMEM((PX, LANES), F32),
        pltpu.VMEM((R, C, 2 * LANES), BF16),
        compact, compact, compact, compact,
        pltpu.VMEM((C, LANES), F32),
        big, big, big, big, big, big, big, big, big, big,
        pltpu.VMEM((2, HALF, WIDE), F32),
        pltpu.VMEM((2, 2, HALF, WIDE), F32),
        pltpu.VMEM((NX, 2, 8, WIDE), F32),
        pltpu.VMEM((NX, 2, 8, WIDE), F32),
        pltpu.VMEM((2, NX, 8, E), F32),
        pltpu.VMEM((2, NX, 8, E), F32),
        pltpu.VMEM((2, 8, WIDE), F32),
        pltpu.VMEM((NZ, 8, WIDE), F32),
        pltpu.VMEM((2, NX, 8, E), F32),
        pltpu.VMEM((2, NX, 8, E), F32),
        pltpu.VMEM((2, HALF, E), F32),
        pltpu.VMEM((2, 2, HALF, E), F32),
        pltpu.VMEM((2, HALF, E), F32),
        pltpu.VMEM((2, R, WIDE), F32),
        pltpu.VMEM((NCOL, R, WIDE), F32),
        pltpu.VMEM((R, PART, E), BF16),
        pltpu.SemaphoreType.DMA((7,)),
        pltpu.SemaphoreType.DMA((N_SEM,)),
        pltpu.SemaphoreType.DMA((N_SEM,)),
        pltpu.SemaphoreType.REGULAR((2,)),
    ]
    return pl.pallas_call(
        kernel,
        out_shape=pltpu.VMEM((R, C, D), BF16),
        in_specs=[hbm] * 7,
        out_specs=vmem,
        scratch_shapes=scratch,
        compiler_params=pltpu.CompilerParams(
            collective_id=0, has_side_effects=True, vmem_limit_bytes=60 * 1024 * 1024),
    )(xin, gate_in, w_proj, rate, skip.reshape(1, E), norm_gain.reshape(1, E), w_out)


def solution(mesh):
    in_specs = (P("rows", "cols", None), P("rows", "cols", None), P(), P(), P(), P(), P())
    return jax.shard_map(local, mesh=mesh, in_specs=in_specs, out_specs=P("rows", "cols", None), check_vma=False)
```

```python
import functools

import jax
import jax.numpy as jnp
from jax import lax
from jax.experimental import pallas as pl
from jax.experimental.pallas import tpu as pltpu
from jax.sharding import PartitionSpec as P

MESH = pl.DeviceIdType.MESH
F32 = jnp.float32
BF16 = jnp.bfloat16

R, C, E, D, HEADS = 8, 64, 1024, 512, 16
PX = R * C
HALF = C // 2
LANES = 128
PART = 16
TILES = E // LANES
WIDE = E + LANES
NB = 256
CHUNKS = E // NB
ZERO_ROW = 112
RS = 72

NZ, NX, NCORE, NCOL = 4, 4, 2, 8
FAR_FIRST = (1, 0, 2)

S_CORE, S_X, S_COLS, S_Z, S_BACK, S_LAST, N_SEM = 0, 2, 8, 15, 18, 24, 27


def split(v):
    hi = v.astype(BF16)
    lo = (v - hi.astype(F32)).astype(BF16)
    return jnp.concatenate([hi, lo], axis=-1)


def mxu(a, b):
    return jnp.dot(a, b, preferred_element_type=F32)


def kernel(x_hbm, g_hbm, wp_hbm, rate_hbm, skip_hbm, gain_hbm, wo_hbm, ob,
           xb, gb, wp, wo, rate_ref, skip_ref, gain_ref, zsel, c1f, v_hl, d_hl, c1_hl, l_hl, h_hl, fv,
           base, ro2, ro3, gg, hd0, hb0, ho0, hd1, hb1, ho1,
           s0, ee, tt, xe, px, gx, tz, ze, sc, rc, fxp, cc, pc, he, hr, nb,
           lsem, ssem, rsem, gsem):
    rows = lax.axis_index("rows")
    col = lax.axis_index("cols")
    core = rows % NCORE
    xi = (rows // NCORE) % NX
    zi = rows // (NCORE * NX)

    core_peer = {"rows": rows + 1 - 2 * core}
    x_dst = [(xi + d) % NX for d in range(1, NX)]
    x_peers = [{"rows": (zi * NX + t) * NCORE + core} for t in x_dst]
    z_peers = [{"rows": (((zi + d) % NZ) * NX + xi) * NCORE + core} for d in range(1, NZ)]
    c_peers = [{"cols": (col + d) % NCOL} for d in range(1, NCOL)]
    def greeter(peer):
        peer_rows = peer.get("rows", rows)
        return {"rows": peer_rows - peer_rows % NCORE + 1, "cols": peer.get("cols", col)}

    outside = [greeter(peer) for peer in x_peers + z_peers + c_peers]
    barrier = pltpu.get_barrier_semaphore()

    @pl.when(core == 1)
    def _():
        pl.semaphore_signal(barrier, inc=1, device_id=core_peer, device_id_type=MESH)

    for peer in outside:
        pl.semaphore_signal(barrier, inc=1, device_id=peer, device_id_type=MESH)

    def wait_for_core():
        @pl.when(core == 0)
        def _():
            pl.semaphore_wait(barrier, 1)
            pl.semaphore_signal(gsem.at[0], inc=1, device_id=core_peer, device_id_type=MESH)

        @pl.when(core == 1)
        def _():
            pl.semaphore_wait(gsem.at[0], 1)

    def wait_for_others():
        @pl.when(core == 1)
        def _():
            pl.semaphore_wait(barrier, NCORE * len(outside))
            pl.semaphore_signal(gsem.at[1], inc=1, device_id=core_peer, device_id_type=MESH)

        @pl.when(core == 0)
        def _():
            pl.semaphore_wait(gsem.at[1], 1)

    load_wp = pltpu.make_async_copy(wp_hbm, wp, lsem.at[0])
    load_x = pltpu.make_async_copy(x_hbm, xb, lsem.at[1])
    load_g = pltpu.make_async_copy(g_hbm, gb, lsem.at[2])
    load_wo = pltpu.make_async_copy(wo_hbm, wo, lsem.at[3])
    load_rate = pltpu.make_async_copy(rate_hbm, rate_ref, lsem.at[4])
    load_skip = pltpu.make_async_copy(skip_hbm, skip_ref, lsem.at[5])
    load_gain = pltpu.make_async_copy(gain_hbm, gain_ref, lsem.at[6])
    load_wp.start()
    load_x.start()
    load_rate.start()
    load_skip.start()
    load_gain.start()
    load_g.start()
    load_wo.start()

    def remote(src, dst, number, peer):
        return pltpu.make_async_remote_copy(
            src_ref=src, dst_ref=dst, send_sem=ssem.at[number], recv_sem=rsem.at[number],
            device_id=peer, device_id_type=MESH)

    zsel[...] = jnp.zeros_like(zsel)
    head_row = lax.broadcasted_iota(jnp.int32, (HEADS, E), 0)
    head_col = lax.broadcasted_iota(jnp.int32, (HEADS, E), 1) // (E // HEADS)
    zsel[ZERO_ROW:ZERO_ROW + HEADS, :] = (head_row == head_col).astype(F32).astype(BF16)

    def sel(off, cols):
        part = zsel[ZERO_ROW - off:ZERO_ROW - off + LANES, cols]
        return jnp.concatenate([part, part], axis=0)

    def chunk(n):
        return pl.ds(pl.multiple_of(n * NB, NB), NB)

    def spread(v, off):
        return mxu(split(v), sel(off, slice(0, E)))

    low = lax.broadcasted_iota(jnp.int32, (8, LANES), 1) < 64

    def spread_few(v, off):
        out = []
        for m in range(v.shape[0] // 8):
            row = v[m * 8:(m + 1) * 8]
            tiles = []
            for t in range(TILES):
                a = jnp.broadcast_to(row[:, off + 2 * t:off + 2 * t + 1], (8, LANES))
                b = jnp.broadcast_to(row[:, off + 2 * t + 1:off + 2 * t + 2], (8, LANES))
                tiles.append(jnp.where(low, a, b))
            out.append(jnp.concatenate(tiles, axis=1))
        return jnp.concatenate(out, axis=0)

    src_lane = lax.broadcasted_iota(jnp.int32, (LANES, 2 * LANES), 0)
    lane = lax.broadcasted_iota(jnp.int32, (LANES, 2 * LANES), 1)
    within = lane % 64
    h = within % 16
    want = 32 * (within // 16) + jnp.where(lane < 128, h, jnp.where(lane < 192, 16 + h // 2, 24 + h // 2))
    pick = (src_lane == want).astype(F32).astype(BF16)
    load_wp.wait()
    w2 = mxu(wp[...], pick).astype(BF16)
    load_rate.wait()
    rate = rate_ref[...]
    rate_lane = jnp.concatenate([rate[k:k + 1, :] for k in range(4)] * 2, axis=1)
    load_x.wait()
    proj = mxu(xb[...].reshape(PX, E), w2)
    pre = proj[:, :LANES]
    coef = proj[:, LANES:]
    step = jnp.maximum(pre, 0.0) + jnp.log1p(jnp.exp(-jnp.abs(pre)))
    logd = -rate_lane * step
    lane1 = lax.broadcasted_iota(jnp.int32, (PX, LANES), 1)
    c1 = jnp.where(lane1 < 64, step * coef, coef)
    c1f[...] = c1
    l_hl[...] = split(logd)
    d_hl[...] = split(jnp.exp(logd))
    c1_hl[...] = split(c1)

    logr = [logd[r * C:(r + 1) * C, :] for r in range(R)]
    up = [logr[0]]
    for r in range(1, R):
        up.append(up[-1] + logr[r])
    down = [logr[R - 1]]
    for r in range(R - 2, -1, -1):
        down.insert(0, down[0] + logr[r])
    zero = jnp.zeros((C, LANES), F32)
    lane2 = lax.broadcasted_iota(jnp.int32, (C, LANES), 1)
    falling = (lane2 % 64) >= 48
    for r in range(R):
        before = up[r - 1] if r else zero
        after = down[r + 1] if r < R - 1 else zero
        tail = jnp.where(falling, before, after)
        reach = jnp.where(falling, down[r], up[r])
        v = jnp.exp(jnp.where(lane2 < 64, tail, reach)) * c1[r * C:(r + 1) * C, :]
        v_hl[r] = split(v)
    fv[...] = jnp.exp(up[R - 1])

    def column_ends(start, i, dst):
        lhs = v_hl[:, pl.ds(start, HALF), :].reshape(R * HALF, 2 * LANES)
        for n in range(CHUNKS):
            cs = slice(n * NB, (n + 1) * NB)
            w = mxu(lhs, sel(32 + 16 * i, cs))
            acc = w[:HALF] * xb[0, pl.ds(start, HALF), cs].astype(F32)
            for r in range(1, R):
                acc = acc + w[r * HALF:(r + 1) * HALF] * xb[r, pl.ds(start, HALF), cs].astype(F32)
            dst[i, :, cs] = acc
        dst[i, :, E:] = fv[pl.ds(start, HALF), :]

    own = pl.multiple_of(core * HALF, HALF)
    other = pl.multiple_of((1 - core) * HALF, HALF)
    to_core = [remote(s0.at[i], ee.at[core, i], S_CORE + i, core_peer) for i in range(2)]
    column_ends(other, 1, s0)

    wait_for_core()
    to_core[1].start()
    column_ends(other, 0, s0)
    to_core[0].start()
    column_ends(own, 1, ee.at[core])
    column_ends(own, 0, ee.at[core])


    bt = lax.broadcasted_iota(jnp.int32, (256, 256), 0)
    bs = lax.broadcasted_iota(jnp.int32, (256, 256), 1)
    same = (bt // C) == (bs // C)
    behind = (same & (bs > bt)).astype(F32).astype(BF16)
    ahead = (same & (bs < bt)).astype(F32).astype(BF16)
    lane3 = lax.broadcasted_iota(jnp.int32, (256, LANES), 1)
    for m in range(PX // 256):
        ps = slice(m * 256, (m + 1) * 256)
        lh = l_hl[ps, :]
        a = mxu(behind, lh)
        b = mxu(ahead, lh)
        cum = jnp.where(lane3 < 16, a[:, :LANES] + a[:, LANES:], b[:, :LANES] + b[:, LANES:])
        h_hl[ps, :] = split(jnp.exp(cum) * c1f[ps, :])
    row_of = lax.broadcasted_iota(jnp.int32, (R, PX), 1) // C
    whole = (row_of == lax.broadcasted_iota(jnp.int32, (R, PX), 0)).astype(F32).astype(BF16)
    ft = mxu(whole, l_hl[...])
    ft = jnp.exp(ft[:, :LANES] + ft[:, LANES:])

    first = (NZ - zi) // NZ
    r_early = CHUNKS * ((NZ - 1 - zi) // (NZ // 2))
    c_early = CHUNKS // 2 * (first + (NZ - 1 - zi) // (NZ // 2))
    g_early = CHUNKS * first

    def row_ends(n, _):
        cs = chunk(n)
        for i in range(2):
            w = mxu(h_hl[...], sel(16 * i, cs)).reshape(R, C, NB)
            he[i, :, cs] = jnp.sum(w * xb[:, :, cs].astype(F32), axis=1)
        return 0

    lax.fori_loop(0, r_early, row_ends, 0)
    for i in range(2):
        he[i, :, E:] = ft

    load_skip.wait()
    load_gain.wait()

    def column_scans(n, _):
        cs = chunk(n)
        xs = [xb[r, :, cs].astype(F32) for r in range(R)]
        sk = skip_ref[:, cs]
        acc = [sk * xs[r] for r in range(R)]
        for i in range(2):
            off = 32 + 16 * i
            dd = mxu(d_hl[...], sel(off, cs))
            bb = mxu(c1_hl[...], sel(off, cs))
            oo = mxu(c1_hl[...], sel(64 + off, cs))
            state = None
            for r in (range(R) if i == 0 else range(R - 1, -1, -1)):
                ps = slice(r * C, (r + 1) * C)
                push = bb[ps] * xs[r]
                state = push if state is None else dd[ps] * state + push
                acc[r] = acc[r] + oo[ps] * state
        for r in range(R):
            for t in range(2):
                base[2 * n + t, r * RS:r * RS + C, :] = acc[r][:, t * LANES:(t + 1) * LANES]
        return 0

    lax.fori_loop(0, c_early, column_scans, 0)
    load_g.wait()
    load_wo.wait()

    def gates(n, _):
        cs = chunk(n)
        gain = gain_ref[:, cs]
        for r in range(R):
            g = gb[r, :, cs].astype(F32)
            w = gain * (g / (1.0 + jnp.exp(-g)))
            for t in range(2):
                gg[2 * n + t, r * RS:r * RS + C, :] = w[:, t * LANES:(t + 1) * LANES]
        return 0

    lax.fori_loop(0, g_early, gates, 0)

    to_x = [[remote(tt.at[x_dst[d], i], xe.at[xi, i], S_X + 3 * i + d, x_peers[d]) for d in range(NX - 1)]
            for i in range(2)]

    def join_cores(i):
        to_core[i].wait_recv()
        first, second = ee.at[i, i], ee.at[1 - i, i]
        t = second[:, :E] + spread_few(second[:, E:], 32 + 16 * i) * first[:, :E]
        f = second[:, E:] * first[:, E:]
        for q in range(NX):
            tt[q, i, :, :E] = t[q * 8:(q + 1) * 8]
            tt[q, i, :, E:] = f[q * 8:(q + 1) * 8]
        if i == 1:
            wait_for_others()
        for d in FAR_FIRST:
            to_x[i][d].start()
        xe[xi, i] = tt[xi, i]

    join_cores(1)
    lax.fori_loop(r_early, CHUNKS, row_ends, 0)
    to_cols = [remote(he.at[(col + d) // NCOL], hr.at[col], S_COLS + d - 1, c_peers[d - 1])
               for d in range(1, NCOL)]
    for copy in to_cols:
        copy.start()
    hr[col] = he[0]

    join_cores(0)
    lax.fori_loop(c_early, CHUNKS, column_scans, 0)


    def reach_spread(n, _):
        cs = chunk(n)
        vv = v_hl[...].reshape(PX, 2 * LANES)
        for off, dst in ((96, ro2), (112, ro3)):
            w = mxu(vv, sel(off, cs))
            for r in range(R):
                for t in range(2):
                    dst[2 * n + t, r * RS:r * RS + C, :] = w[r * C:(r + 1) * C, t * LANES:(t + 1) * LANES]
        return 0

    lax.fori_loop(g_early, r_early, gates, 0)
    lax.fori_loop(0, r_early, reach_spread, 0)

    def row_spread(n, _):
        cs = chunk(n)
        dv = d_hl[...]
        cv = c1_hl[...]
        xs = xb[:, :, cs].astype(F32)
        for lhs, off, drive, dst in ((dv, 0, 0, hd0), (cv, 0, 1, hb0), (cv, 64, 0, ho0),
                                     (dv, 16, 0, hd1), (cv, 16, 1, hb1), (cv, 80, 0, ho1)):
            w = mxu(lhs, sel(off, cs)).reshape(R, C, NB)
            if drive:
                w = w * xs
            for r in range(R):
                for t in range(2):
                    dst[2 * n + t, r * RS:r * RS + C, :] = w[r, :, t * LANES:(t + 1) * LANES]
        return 0

    lax.fori_loop(0, c_early, row_spread, 0)

    to_z = [remote(tz.at[(zi + d) // NZ], ze.at[zi], S_Z + d - 1, z_peers[d - 1]) for d in range(1, NZ)]
    for i in (1, 0):
        for copy in to_x[i]:
            copy.wait_recv()
        fc = xe[0, i, :, E:]
        for q in range(1, NX):
            fc = fc * xe[q, i, :, E:]
        fs = spread_few(xe[:, i, :, E:].reshape(NX * 8, LANES), 32 + 16 * i)
        acc = jnp.zeros((8, E), F32)
        g = jnp.ones((8, E), F32)
        for q in (range(NX) if i == 0 else range(NX - 1, -1, -1)):
            f = fs[q * 8:(q + 1) * 8]
            px[i, q] = acc
            gx[i, q] = g
            acc = xe[q, i, :, :E] + f * acc
            g = g * f
        tz[i, :, :E] = acc
        tz[i, :, E:] = pltpu.roll(fc, LANES - 32 - 16 * i, 1)
        for d in FAR_FIRST:
            @pl.when((zi + d + 1) // NZ == i)
            def _():
                to_z[d].start()
    ze[zi] = tz[0]

    for i in range(2):
        fxp[i] = spread(ee[i, i, :, E:], 32 + 16 * i)

    def back_copies(i, order):
        return [remote(sc.at[i, x_dst[d]], rc.at[i, xi], S_BACK + 3 * order + d, x_peers[d]) for d in range(NX - 1)]

    def over_groups(i, order):
        for d in range(1, NZ):
            @pl.when(1 - (zi + NZ - d) // NZ == i)
            def _():
                to_z[d - 1].wait_recv()
        before = zi + i * (NZ - 1 - 2 * zi)
        slots = []
        for m in range(NZ - 1):
            valid = (before + NZ - 1 - m) // NZ
            slots.append(valid * (m + i * (NZ - 1 - 2 * m)) + (1 - valid) * zi)
        fs = spread_few(jnp.concatenate([ze[j, :, E:] for j in slots], axis=0), 0)
        acc = jnp.zeros((8, E), F32)
        for m, j in enumerate(slots):
            acc = jnp.where(m < before, ze[j, :, :E] + fs[m * 8:(m + 1) * 8] * acc, acc)
        for q in range(NX):
            sc[i, q] = px[i, q] + gx[i, q] * acc
        copies = back_copies(i, order)
        for d in FAR_FIRST:
            copies[d].start()
        rc[i, xi] = sc[i, xi]

    def to_last(i, order):
        return remote(cc.at[1 - core, i], pc.at[i], S_LAST + order, core_peer)

    def over_chip(i, order):
        for copy in back_copies(i, order):
            copy.wait_recv()
        carry = rc[i].reshape(HALF, E)
        cc[i, i] = carry
        cc[1 - i, i] = ee[i, i, :, :E] + fxp[i] * carry
        to_last(i, order).start()

    near = zi // (NZ // 2)
    far = 1 - near

    edge = zi % (NZ - 1) == 0

    @pl.when(edge)
    def _():
        over_groups(near, 0)

    lax.fori_loop(c_early, CHUNKS, row_spread, 0)
    for copy in to_cols:
        copy.wait_recv()
    fh = hr[:, :, E:].reshape(NCOL * R, LANES)
    f0 = spread(fh, 0)
    f1 = spread(fh, 16)
    in0 = jnp.zeros((R, E), F32)
    in1 = jnp.zeros((R, E), F32)
    for j in range(NCOL):
        in0 = jnp.where(j < col, hr[j, :, :E] + f0[j * R:(j + 1) * R] * in0, in0)
    for j in range(NCOL - 1, -1, -1):
        in1 = jnp.where(j > col, hr[j, :, :E] + f1[j * R:(j + 1) * R] * in1, in1)

    def row_step(c, states):
        out = []
        for at, hd, hb, ho, first in ((c, hd0, hb0, ho0, 0), (C - 1 - c, hd1, hb1, ho1, TILES)):
            ps = pl.ds(at, R, stride=RS)
            for t in range(TILES):
                s = hd[t, ps, :] * states[first + t] + hb[t, ps, :]
                base[t, ps, :] = base[t, ps, :] + ho[t, ps, :] * s
                out.append(s)
        return tuple(out)

    begin = [in0[:, t * LANES:(t + 1) * LANES] for t in range(TILES)]
    begin += [in1[:, t * LANES:(t + 1) * LANES] for t in range(TILES)]
    states = lax.fori_loop(0, C // 2, row_step, tuple(begin), unroll=2)

    @pl.when(jnp.logical_not(edge))
    def _():
        over_groups(near, 0)

    over_groups(far, 1)
    lax.fori_loop(C // 2, C, row_step, states, unroll=2)
    lax.fori_loop(r_early, CHUNKS, gates, 0)
    lax.fori_loop(r_early, CHUNKS, reach_spread, 0)
    over_chip(near, 0)

    odd = xi % 2

    def arrived(d):
        remote(sc.at[far, xi], rc.at[far, xi], S_BACK + 3 + d, x_peers[1]).wait_recv()

    def last_part(p):
        cs = pl.ds(starts[p], PART)
        return remote(cc.at[1 - core, far, cs], pc.at[far, cs], S_LAST + 1 + p, core_peer)

    def over_chip_part(p):
        cs = pl.ds(starts[p], PART)
        carry = rc[far, pl.ds(starts[p] // 8, PART // 8)].reshape(PART, E)
        cc[far, far, cs, :] = carry
        cc[1 - far, far, cs, :] = ee[far, far, cs, :E] + fxp[far, cs, :] * carry
        last_part(p).start()

    group = xi // 2
    starts = [pl.multiple_of(group * PART, PART), pl.multiple_of((1 - group) * PART, PART)]

    def finish(start, carry, p):
        cs = pl.ds(starts[p], PART)
        for r in range(R):
            ps = pl.ds(pl.multiple_of(r * RS + start + starts[p], 8), PART)
            tot = []
            sq = jnp.zeros((PART, LANES), F32)
            for t in range(TILES):
                ls = slice(t * LANES, (t + 1) * LANES)
                v = base[t, ps, :] + ro2[t, ps, :] * carry[0, cs, ls] + ro3[t, ps, :] * carry[1, cs, ls]
                sq = sq + v * v
                tot.append(v)
            scale = lax.rsqrt(jnp.sum(sq, axis=-1, keepdims=True) * (1.0 / E) + 1e-05)
            for t in range(TILES):
                ls = slice(t * LANES, (t + 1) * LANES)
                nb[r, :, ls] = (tot[t] * scale * gg[t, ps, :]).astype(BF16)
        res = mxu(nb[...].reshape(R * PART, E), wo[...])
        at = pl.multiple_of(start + starts[p], PART)
        ob[:, pl.ds(at, PART), :] = res.astype(BF16).reshape(R, PART, D)

    arrived(2 - 2 * odd)
    over_chip_part(0)
    finish(own, cc.at[core], 0)
    arrived(1)
    arrived(2 * odd)
    over_chip_part(1)
    finish(own, cc.at[core], 1)
    to_last(near, 0).wait_recv()
    for p in range(2):
        last_part(p).wait_recv()
        finish(other, pc, p)
    for copy in to_core + to_x[0] + to_x[1] + to_cols + to_z + back_copies(near, 0) + back_copies(far, 1):
        copy.wait_send()
    to_last(near, 0).wait_send()
    for p in range(2):
        last_part(p).wait_send()


def local(xin, gate_in, w_proj, rate, skip, norm_gain, w_out):
    vmem = pl.BlockSpec(memory_space=pltpu.VMEM)
    hbm = pl.BlockSpec(memory_space=pl.ANY)
    big = pltpu.VMEM((TILES, R * RS, LANES), F32)
    compact = pltpu.VMEM((PX, 2 * LANES), BF16)
    scratch = [
        pltpu.VMEM((R, C, E), BF16),
        pltpu.VMEM((R, C, E), BF16),
        pltpu.VMEM((E, LANES), BF16),
        pltpu.VMEM((E, D), BF16),
        pltpu.VMEM((4, HEADS), F32),
        pltpu.VMEM((1, E), F32),
        pltpu.VMEM((1, E), F32),
        pltpu.VMEM((ZERO_ROW + LANES, E), BF16),
        pltpu.VMEM((PX, LANES), F32),
        pltpu.VMEM((R, C, 2 * LANES), BF16),
        compact, compact, compact, compact,
        pltpu.VMEM((C, LANES), F32),
        big, big, big, big, big, big, big, big, big, big,
        pltpu.VMEM((2, HALF, WIDE), F32),
        pltpu.VMEM((2, 2, HALF, WIDE), F32),
        pltpu.VMEM((NX, 2, 8, WIDE), F32),
        pltpu.VMEM((NX, 2, 8, WIDE), F32),
        pltpu.VMEM((2, NX, 8, E), F32),
        pltpu.VMEM((2, NX, 8, E), F32),
        pltpu.VMEM((2, 8, WIDE), F32),
        pltpu.VMEM((NZ, 8, WIDE), F32),
        pltpu.VMEM((2, NX, 8, E), F32),
        pltpu.VMEM((2, NX, 8, E), F32),
        pltpu.VMEM((2, HALF, E), F32),
        pltpu.VMEM((2, 2, HALF, E), F32),
        pltpu.VMEM((2, HALF, E), F32),
        pltpu.VMEM((2, R, WIDE), F32),
        pltpu.VMEM((NCOL, R, WIDE), F32),
        pltpu.VMEM((R, PART, E), BF16),
        pltpu.SemaphoreType.DMA((7,)),
        pltpu.SemaphoreType.DMA((N_SEM,)),
        pltpu.SemaphoreType.DMA((N_SEM,)),
        pltpu.SemaphoreType.REGULAR((2,)),
    ]
    return pl.pallas_call(
        kernel,
        out_shape=pltpu.VMEM((R, C, D), BF16),
        in_specs=[hbm] * 7,
        out_specs=vmem,
        scratch_shapes=scratch,
        compiler_params=pltpu.CompilerParams(
            collective_id=0, has_side_effects=True, vmem_limit_bytes=60 * 1024 * 1024),
    )(xin, gate_in, w_proj, rate, skip.reshape(1, E), norm_gain.reshape(1, E), w_out)


def solution(mesh):
    in_specs = (P("rows", "cols", None), P("rows", "cols", None), P(), P(), P(), P(), P())
    return jax.shard_map(local, mesh=mesh, in_specs=in_specs, out_specs=P("rows", "cols", None), check_vma=False)
```
